32 devices in a mesh: gx: 4 (over z), gy: 2 (over y), gz: 4 (over x, core).
Axes of the slice: x: 2, y: 2, z: 4, core: 2. Of those that a mesh axis runs over, the one named last changes fastest.
Arguments:
- amplitudes: bfloat16 [1792, 16384], P(('gz', 'gy'), 'gx'), may hold values from -6 to 6
- virt_integrals: bfloat16 [16384, 16384], P('gx', ('gy', 'gz')), may hold values from -0.046875 to 0.046875
- occ_integrals: bfloat16 [1792, 1792], P('gz'), may hold values from -0.125 to 0.125
- occ_irrep: int32 [1792], P(('gz', 'gy')), may hold values from 0 to 7, as said below
- virt_irrep: int32 [16384], P('gx'), may hold values from 0 to 7, as said below
Outputs:
- ladder_term: float32 [1792, 16384], P(('gz', 'gx'), 'gy')
- hole_term: float32 [1792, 16384], P('gz', ('gx', 'gy'))
The draws below stay inside these ranges and needn't reach their ends.
Inputs may be any that keep to these rules, and one draw needn't show every extreme that they name: `occ_irrep`: labels never fall along the array and come in runs of whole multiples of 64 pairs. `virt_irrep`: labels never fall along the array and come in runs of whole multiples of 64 pairs.
All inputs are finite; a program needn't handle non-finite values.
Results may differ from the reference program's by a relative error of at most 0.0003.
Values may be sent and summed in bfloat16 or wider, within the bound.
No kernel may reach another device: no remote copies, remote signals or barrier semaphores. Data moves between devices by JAX's collectives and lax.ppermute only.
A program may use at most 192 MiB of HBM per device.

```python
import jax
import jax.numpy as jnp
from jax import lax

OP = 1792
VP = 16384
NIR = 8
IRB = 64


def unit_labels(key, tag, units):
    drawn = jax.random.randint(jax.random.fold_in(key, tag), (units,), 0, 3 * NIR).astype(jnp.int32)
    return jnp.where(drawn < NIR, drawn, jnp.zeros_like(drawn))


def draw_occ_irrep(key, part):
    labels = jnp.sort(unit_labels(key, 11, OP // IRB))
    return jnp.repeat(labels, IRB, total_repeat_length=OP).astype(jnp.int32)


def draw_virt_irrep(key, part):
    labels = jnp.sort(unit_labels(key, 13, VP // IRB))
    return jnp.repeat(labels, IRB, total_repeat_length=VP).astype(jnp.int32)


def strengthened(result, rng, source, target, blocks, factor):
    owner, partner = [(jnp.arange(result.shape[position]) // (result.shape[position] // blocks)).reshape([-1 if axis == position else 1 for axis in range(result.ndim)]) for position in (source, target)]
    chosen = jax.random.permutation(rng, blocks)[partner]
    strong = (owner == chosen) | (owner == (partner + blocks // 2) % blocks)
    return jnp.where(strong, factor * result, result)


def levels(key, extent, cuts, smallest, top_value):
    def one(position, parts):
        draws = jax.random.uniform(jax.random.fold_in(jax.random.fold_in(key, 6), position), (parts,), jnp.float32, smallest / len(cuts), top_value / len(cuts))
        return jnp.repeat(jnp.exp(draws), extent[position] // parts).reshape((-1,) + (1,) * (len(extent) - position - 1))

    factor_of = one(*cuts[0])
    for cut in cuts[1:]:
        factor_of = factor_of * one(*cut)
    return factor_of


def normal_values(own_key, extent, deviation, limit, shards=(), kind=jnp.bfloat16):
    factor_of = levels(own_key, extent, shards, -0.22, 0.18) if shards else 1.0
    array = jax.random.normal(own_key, extent, jnp.float32) * deviation * factor_of
    return jnp.minimum(jnp.maximum(array, -limit), limit).astype(kind)


def noise_with(own_key, shape, deviation, bound, cuts, heavy, kind=jnp.bfloat16):
    values = deviation * jax.random.normal(own_key, shape, jnp.float32)
    if cuts:
        values = values * levels(own_key, shape, cuts, -0.22, 0.18)
    return jnp.clip(strengthened(values, jax.random.fold_in(own_key, 3), *heavy), -bound, bound).astype(kind)


def setup_inputs(seed: int = 0) -> dict:
    key_list = jax.random.split(jax.random.key(seed), 6)
    return {
        "amplitudes": noise_with(key_list[0], (OP, VP), 1.0, 6.0, ((0, 8), (1, 4)), (1, 0, 8, 2.0)),
        "virt_integrals": normal_values(key_list[1], (VP, VP), VP ** -0.5, 0.046875, ((0, 4), (1, 8))),
        "occ_integrals": normal_values(key_list[2], (OP, OP), OP ** -0.5, 0.125, ((0, 4),)),
        "occ_irrep": draw_occ_irrep(jax.random.fold_in(key_list[5], 71), 0),
        "virt_irrep": draw_virt_irrep(jax.random.fold_in(key_list[5], 71), 0),
    }


def reference(amplitudes, virt_integrals, occ_integrals, occ_irrep, virt_irrep):
    keep = occ_irrep[:, None] == virt_irrep[None, :]
    masked = jnp.where(keep, amplitudes, jnp.zeros_like(amplitudes)).astype(jnp.bfloat16)
    masked_wide = masked.astype(jnp.float32)
    block_width = min(VP, 1024)
    count = VP // block_width

    def one_block(index_block):
        start = (index_block * block_width).astype(jnp.int32)
        columns = lax.dynamic_slice_in_dim(virt_integrals, start, block_width, 1).astype(jnp.float32)
        return jnp.dot(masked_wide, columns, precision=lax.Precision.HIGHEST)

    blocks = lax.map(one_block, jnp.arange(count, dtype=jnp.int32))
    ladder_term = jnp.transpose(blocks, (1, 0, 2)).reshape(OP, VP)
    hole_term = jnp.dot(occ_integrals, masked, preferred_element_type=jnp.float32)
    return ladder_term, hole_term
```

```python
import jax
import jax.numpy as jnp
from jax import lax
from jax.sharding import PartitionSpec as P

F32 = jnp.float32
WIRE = jnp.float16
TOP = 32768.0


def masked_rows(amplitudes, occ_irrep, virt_irrep):
    keep = occ_irrep[:, None] == virt_irrep[None, :]
    return jnp.where(keep, amplitudes, jnp.zeros_like(amplitudes))


def whole_sums(amplitudes, virt_integrals, occ_integrals, occ_irrep, virt_irrep):
    masked = masked_rows(amplitudes, occ_irrep, virt_irrep)
    rows = lax.all_gather(masked, ("gz", "gy"), axis=0, tiled=True)
    partial = jnp.dot(rows, virt_integrals, preferred_element_type=F32)
    nx, nz = lax.axis_size("gx"), lax.axis_size("gz")
    by_owner = partial.reshape(nz, nx, -1, partial.shape[1]).swapaxes(0, 1)
    mine = lax.psum_scatter(by_owner, "gx", scatter_dimension=0, tiled=True)
    ladder_term = lax.all_to_all(mine[0], "gz", split_axis=0, concat_axis=2, tiled=True)[0]
    width = rows.shape[1] // lax.axis_size("gy")
    columns = lax.dynamic_slice_in_dim(rows, lax.axis_index("gy") * width, width, 1)
    hole_term = jnp.dot(occ_integrals, columns, preferred_element_type=F32)
    return ladder_term, hole_term


def line_of_four(amplitudes, virt_integrals, occ_integrals, occ_irrep, virt_irrep):
    z, y, g = (lax.axis_index(name) for name in ("gx", "gy", "gz"))
    mirrored = z >= 2
    first = (y == 1) != mirrored
    inner = (z == 1) | (z == 2)
    part = amplitudes.shape[0] // 2
    cols = virt_integrals.shape[1]

    def over_gz(value, flip):
        return lax.ppermute(value, "gz", [(i, i ^ flip) for i in range(4)])

    def over_gy(value):
        return lax.ppermute(value, "gy", [(0, 1), (1, 0)])

    def over_gx(packed, pairs):
        return tuple(lax.ppermute(item, "gx", pairs) for item in packed)

    def own_part(start):
        rows = lax.dynamic_slice_in_dim(amplitudes, start, part, 0)
        labels = lax.dynamic_slice_in_dim(occ_irrep, start, part, 0)
        return masked_rows(rows, labels, virt_irrep)

    def pick(condition, one, other):
        return jnp.where(condition, one, other)

    def pair(value):
        return jnp.concatenate([value, over_gz(value, 1)], axis=0)

    odd = pick(mirrored, 0, part)
    high, low = own_part(odd), own_part(part - odd)

    y_high = over_gy(high)
    x_high = over_gz(high, 2)
    high_near = pair(high)
    y_low = over_gy(low)
    y_high_near = pair(y_high)
    yx_high = over_gz(y_high, 2)
    high_far = pair(x_high)
    two, zero = pick(first, low, y_low), pick(first, y_low, low)
    x_two = over_gz(two, 2)
    two_near, zero_near = pair(two), pair(zero)
    y_high_far = pair(yx_high)
    two_far = pair(x_two)
    x_zero = over_gz(zero, 2)
    zero_far = pair(x_zero)

    def product(rows):
        return jnp.dot(rows, virt_integrals, preferred_element_type=F32)

    def pack(value):
        top = jnp.maximum(jnp.max(jnp.abs(value)), 1e-30)
        return (value * (TOP / top)).astype(WIRE), (top * (1.0 / TOP)).reshape(1)

    def unpack(packed):
        return packed[0].astype(F32) * packed[1]

    out_pairs, mid_pairs, in_pairs = [(0, 1), (3, 2)], [(1, 2), (2, 1)], [(2, 3), (1, 0)]

    p_high_near = product(high_near)
    a0 = over_gx(pack(p_high_near), out_pairs)
    p_high_far = product(high_far)
    p_y_high_near = product(y_high_near)
    a1 = over_gx(pack(pick(first, p_high_far, p_y_high_near)), out_pairs)
    p_y_high_far = product(y_high_far)
    a2 = over_gx(pack(pick(first, p_y_high_near, p_y_high_far)), out_pairs)
    p_two_far = product(two_far)
    a3 = over_gx(pack(p_two_far), out_pairs)
    a4 = over_gx(pack(pick(first, p_y_high_far, p_high_far)), out_pairs)
    p_two_near = product(two_near)
    a5 = over_gx(pack(p_two_near), out_pairs)
    p_zero_near = product(zero_near)
    p_zero_far = product(zero_far)

    got0, got1, got2, got3, got4, got5 = (unpack(item) for item in (a0, a1, a2, a3, a4, a5))
    b0 = over_gx(pack(pick(first, got0, got1) + pick(first, p_high_near, p_y_high_near)), mid_pairs)
    b1 = over_gx(pack(pick(first, got1, got2) + pick(first, p_high_far, p_y_high_far)), mid_pairs)
    b2 = over_gx(pack(got3 + p_two_far), mid_pairs)
    b3 = over_gx(pack(got5 + p_two_near), mid_pairs)
    c0 = over_gx(pack(unpack(b0) + p_zero_near), in_pairs)
    c1 = over_gx(pack(unpack(b1) + p_zero_far), in_pairs)

    base_near = pick(inner, pick(first, p_y_high_near, p_high_near), p_zero_near)
    base_far = pick(inner, pick(first, p_y_high_far, p_high_far), p_zero_far)
    total_near = base_near + pick(first, got2, got0) + unpack(b3) + unpack(c0)
    total_far = base_far + got4 + unpack(b2) + unpack(c1)

    blocks = [
        total_near[:part],
        over_gz(total_near[part:], 1),
        over_gz(total_far[:part], 2),
        over_gz(total_far[part:], 3),
    ]
    ladder_term = jnp.zeros((part, 4 * cols), F32)
    for flip, block in enumerate(blocks):
        ladder_term = lax.dynamic_update_slice(ladder_term, block, (0, (g ^ flip) * cols))

    width = amplitudes.shape[1] // 2
    columns = jnp.zeros((16 * part, width), amplitudes.dtype)

    def owner(index):
        return pick(mirrored, 3 - index, index)

    held = (
        (owner(pick(first, 3, 1)), high_near, high_far),
        (owner(pick(first, 1, 3)), y_high_near, y_high_far),
        (owner(2), two_near, two_far),
        (owner(0), zero_near, zero_far),
    )
    for place, near, far in held:
        for flip, block in enumerate((near[:part], near[part:], far[:part], far[part:])):
            piece = lax.dynamic_slice_in_dim(block, y * width, width, 1)
            columns = lax.dynamic_update_slice(columns, piece, (((g ^ flip) * 4 + place) * part, 0))
    hole_term = jnp.dot(occ_integrals, columns, preferred_element_type=F32)
    return ladder_term, hole_term


def solution(mesh):
    placed = (P(("gz", "gy"), "gx"), P("gx", ("gy", "gz")), P("gz", None), P(("gz", "gy")), P("gx"))
    sizes = tuple(mesh.shape[name] for name in ("gx", "gy", "gz"))
    return jax.shard_map(
        line_of_four if sizes == (4, 2, 4) else whole_sums,
        mesh=mesh,
        in_specs=placed,
        out_specs=(P(("gz", "gx"), "gy"), P("gz", ("gx", "gy"))),
        check_vma=False,
    )
```

```python
import jax
import jax.numpy as jnp
from jax import lax
from jax.sharding import PartitionSpec as P

F32 = jnp.float32
WIRE = jnp.float16
TOP = 32768.0


def masked_rows(amplitudes, occ_irrep, virt_irrep):
    keep = occ_irrep[:, None] == virt_irrep[None, :]
    return jnp.where(keep, amplitudes, jnp.zeros_like(amplitudes))


def whole_sums(amplitudes, virt_integrals, occ_integrals, occ_irrep, virt_irrep):
    masked = masked_rows(amplitudes, occ_irrep, virt_irrep)
    rows = lax.all_gather(masked, ("gz", "gy"), axis=0, tiled=True)
    partial = jnp.dot(rows, virt_integrals, preferred_element_type=F32)
    nx, nz = lax.axis_size("gx"), lax.axis_size("gz")
    by_owner = partial.reshape(nz, nx, -1, partial.shape[1]).swapaxes(0, 1)
    mine = lax.psum_scatter(by_owner, "gx", scatter_dimension=0, tiled=True)
    ladder_term = lax.all_to_all(mine[0], "gz", split_axis=0, concat_axis=2, tiled=True)[0]
    width = rows.shape[1] // lax.axis_size("gy")
    columns = lax.dynamic_slice_in_dim(rows, lax.axis_index("gy") * width, width, 1)
    hole_term = jnp.dot(occ_integrals, columns, preferred_element_type=F32)
    return ladder_term, hole_term


def line_of_four(amplitudes, virt_integrals, occ_integrals, occ_irrep, virt_irrep):
    z, y, g = (lax.axis_index(name) for name in ("gx", "gy", "gz"))
    mirrored = z >= 2
    first = (y == 1) != mirrored
    inner = (z == 1) | (z == 2)
    part = amplitudes.shape[0] // 2
    cols = virt_integrals.shape[1]

    def over_gz(value, flip):
        return lax.ppermute(value, "gz", [(i, i ^ flip) for i in range(4)])

    def over_gy(value):
        return lax.ppermute(value, "gy", [(0, 1), (1, 0)])

    def over_gx(packed, pairs):
        return tuple(lax.ppermute(item, "gx", pairs) for item in packed)

    def own_part(start):
        rows = lax.dynamic_slice_in_dim(amplitudes, start, part, 0)
        labels = lax.dynamic_slice_in_dim(occ_irrep, start, part, 0)
        return masked_rows(rows, labels, virt_irrep)

    def pick(condition, one, other):
        return jnp.where(condition, one, other)

    def pair(value):
        return jnp.concatenate([value, over_gz(value, 1)], axis=0)

    odd = pick(mirrored, 0, part)
    high, low = own_part(odd), own_part(part - odd)

    y_high = over_gy(high)
    x_high = over_gz(high, 2)
    high_near = pair(high)
    y_low = over_gy(low)
    y_high_near = pair(y_high)
    yx_high = over_gz(y_high, 2)
    high_far = pair(x_high)
    two, zero = pick(first, low, y_low), pick(first, y_low, low)
    x_two = over_gz(two, 2)
    two_near, zero_near = pair(two), pair(zero)
    y_high_far = pair(yx_high)
    two_far = pair(x_two)
    x_zero = over_gz(zero, 2)
    zero_far = pair(x_zero)

    def largest(value):
        return jnp.max(jnp.abs(value)).astype(F32)

    tops = lax.pmax(jnp.stack([largest(amplitudes), largest(virt_integrals)]), ("gx", "gy", "gz"))
    bound = jnp.maximum(tops[0] * tops[1] * (4.0 * virt_integrals.shape[0]), 1e-30)
    up, down = TOP / bound, bound * (1.0 / TOP)

    def product(rows):
        return jnp.dot(rows, virt_integrals, preferred_element_type=F32)

    def send(value, pairs):
        return lax.ppermute((value * up).astype(WIRE), "gx", pairs)

    def got(value):
        return value.astype(F32) * down

    next_in, two_in = [(0, 1), (3, 2)], [(0, 2), (3, 1)]
    middle, next_out, two_out = [(1, 2), (2, 1)], [(2, 3), (1, 0)], [(1, 3), (2, 0)]

    p_high_near = product(high_near)
    a0 = send(p_high_near, next_in)
    p_high_far = product(high_far)
    p_y_high_near = product(y_high_near)
    a1 = send(pick(first, p_high_far, p_y_high_near), next_in)
    p_y_high_far = product(y_high_far)
    a2 = send(pick(first, p_y_high_near, p_y_high_far), next_in)
    far_near = got(pick(first, a0, a1)) + pick(first, p_high_near, p_y_high_near)
    c_near = send(far_near, two_out)
    p_two_near = product(two_near)
    m_near = send(p_two_near, middle)
    p_two_far = product(two_far)
    e_far = send(p_two_far, two_in)
    far_far = got(pick(first, a1, a2)) + pick(first, p_high_far, p_y_high_far)
    c_far = send(far_far, two_out)
    m_far = send(p_two_far, middle)
    a3 = send(pick(first, p_y_high_far, p_high_far), next_in)
    p_zero_far = product(zero_far)
    p_zero_near = product(zero_near)
    o_far = send(p_zero_far, next_out)
    o_near = send(p_zero_near, next_out)
    e_near = send(p_two_near, two_in)

    base_near = pick(inner, pick(first, p_y_high_near, p_high_near), p_zero_near)
    base_far = pick(inner, pick(first, p_y_high_far, p_high_far), p_zero_far)
    total_far = base_far + (got(a3) + got(e_far) + got(m_far)) + (got(c_far) + got(o_far))
    total_near = base_near + (got(pick(first, a2, a0)) + got(e_near) + got(m_near)) + (got(c_near) + got(o_near))

    blocks = [
        total_near[:part],
        over_gz(total_near[part:], 1),
        over_gz(total_far[:part], 2),
        over_gz(total_far[part:], 3),
    ]
    ladder_term = jnp.zeros((part, 4 * cols), F32)
    for flip, block in enumerate(blocks):
        ladder_term = lax.dynamic_update_slice(ladder_term, block, (0, (g ^ flip) * cols))

    width = amplitudes.shape[1] // 2

    def owner(index):
        return pick(mirrored, 3 - index, index)

    held = (
        (owner(pick(first, 3, 1)), high_near, high_far),
        (owner(pick(first, 1, 3)), y_high_near, y_high_far),
        (owner(2), two_near, two_far),
        (owner(0), zero_near, zero_far),
    )
    columns = jnp.zeros((4, 4, part, width), amplitudes.dtype)
    for place, near, far in held:
        rows = jnp.concatenate([near, far], axis=0)
        piece = lax.dynamic_slice_in_dim(rows, y * width, width, 1).reshape(4, 1, part, width)
        columns = lax.dynamic_update_slice(columns, piece, (0, place, 0, 0))
    columns = columns.reshape(16 * part, width)
    by_device = occ_integrals.reshape(occ_integrals.shape[0], 4, 4 * part)
    seen = jnp.concatenate([lax.dynamic_slice_in_dim(by_device, g ^ flip, 1, 1) for flip in range(4)], axis=1)
    hole_term = jnp.dot(seen.reshape(occ_integrals.shape), columns, preferred_element_type=F32)
    return ladder_term, hole_term


def solution(mesh):
    placed = (P(("gz", "gy"), "gx"), P("gx", ("gy", "gz")), P("gz", None), P(("gz", "gy")), P("gx"))
    sizes = tuple(mesh.shape[name] for name in ("gx", "gy", "gz"))
    return jax.shard_map(
        line_of_four if sizes == (4, 2, 4) else whole_sums,
        mesh=mesh,
        in_specs=placed,
        out_specs=(P(("gz", "gx"), "gy"), P("gz", ("gx", "gy"))),
        check_vma=False,
    )
```

```python
import functools

import jax
import jax.numpy as jnp
from jax import lax
from jax.experimental import pallas as pl
from jax.experimental.pallas import tpu as pltpu
from jax.sharding import PartitionSpec as P

F32 = jnp.float32
WIRE = jnp.float16
TOP_EXPONENT = 14.0
EXTRA = 8


def product_kernel(one_ref, other_ref, integrals_ref, out_ref, top_ref, rows_ref):
    part = one_ref.shape[0]

    @pl.when(pl.program_id(0) == 0)
    def _():
        rows_ref[:part] = one_ref[...]
        rows_ref[part:] = other_ref[...]
        top_ref[...] = jnp.zeros_like(top_ref)

    value = jnp.dot(rows_ref[...], integrals_ref[...], preferred_element_type=F32)
    out_ref[...] = value
    size = jnp.abs(value).reshape(-1, *top_ref.shape)
    top_ref[...] = jnp.maximum(top_ref[...], jnp.max(size, axis=0))


def product(one, other, integrals):
    part, depth = one.shape
    cols = integrals.shape[1]
    width = min(cols, 512)
    out, top = pl.pallas_call(
        product_kernel,
        grid=(cols // width,),
        in_specs=[
            pl.BlockSpec((part, depth), lambda j: (0, 0)),
            pl.BlockSpec((part, depth), lambda j: (0, 0)),
            pl.BlockSpec((depth, width), lambda j: (0, j)),
        ],
        out_specs=[pl.BlockSpec((2 * part, width), lambda j: (0, j)), pl.BlockSpec((8, width), lambda j: (0, 0))],
        out_shape=[jax.ShapeDtypeStruct((2 * part, cols), F32), jax.ShapeDtypeStruct((8, width), F32)],
        scratch_shapes=[pltpu.VMEM((2 * part, depth), one.dtype)],
        compiler_params=pltpu.CompilerParams(vmem_limit_bytes=32 << 20),
        cost_estimate=pl.CostEstimate(flops=2_000_000_000, bytes_accessed=2_000_000_000 // 1000, transcendentals=0),
    )(one, other, integrals)
    return out, jnp.max(top)


def hole_kernel(places_ref, *refs):
    *rows_refs, occ_ref, out_ref, columns_ref = refs
    part = rows_refs[0].shape[0]
    for index, rows_ref in enumerate(rows_refs):
        start = pl.multiple_of(places_ref[index] * part, part)
        columns_ref[pl.ds(start, part), :] = rows_ref[...]
    out_ref[...] = jnp.dot(occ_ref[...], columns_ref[...], preferred_element_type=F32)


def hole_product(occ, row_blocks, places, half):
    part, depth = row_blocks[0].shape
    cols = depth // 2
    width = min(cols, 512)
    steps = cols // width
    return pl.pallas_call(
        hole_kernel,
        grid_spec=pltpu.PrefetchScalarGridSpec(
            num_scalar_prefetch=1,
            grid=(steps,),
            in_specs=[pl.BlockSpec((part, width), lambda j, scalars: (0, scalars[len(row_blocks)] * steps + j))] * len(row_blocks)
            + [pl.BlockSpec(occ.shape, lambda j, scalars: (0, 0))],
            out_specs=pl.BlockSpec((occ.shape[0], width), lambda j, scalars: (0, j)),
            scratch_shapes=[pltpu.VMEM((occ.shape[1], width), occ.dtype)],
        ),
        out_shape=jax.ShapeDtypeStruct((occ.shape[0], cols), F32),
        compiler_params=pltpu.CompilerParams(vmem_limit_bytes=32 << 20),
        cost_estimate=pl.CostEstimate(flops=2_000_000_000, bytes_accessed=2_000_000_000 // 1000, transcendentals=0),
    )(jnp.stack([*places, half]).astype(jnp.int32), *row_blocks, occ)


def masked_rows(amplitudes, occ_irrep, virt_irrep):
    keep = occ_irrep[:, None] == virt_irrep[None, :]
    return jnp.where(keep, amplitudes, jnp.zeros_like(amplitudes))


def whole_sums(amplitudes, virt_integrals, occ_integrals, occ_irrep, virt_irrep):
    masked = masked_rows(amplitudes, occ_irrep, virt_irrep)
    rows = lax.all_gather(masked, ("gz", "gy"), axis=0, tiled=True)
    partial = jnp.dot(rows, virt_integrals, preferred_element_type=F32)
    nx, nz = lax.axis_size("gx"), lax.axis_size("gz")
    by_owner = partial.reshape(nz, nx, -1, partial.shape[1]).swapaxes(0, 1)
    mine = lax.psum_scatter(by_owner, "gx", scatter_dimension=0, tiled=True)
    ladder_term = lax.all_to_all(mine[0], "gz", split_axis=0, concat_axis=2, tiled=True)[0]
    width = rows.shape[1] // lax.axis_size("gy")
    columns = lax.dynamic_slice_in_dim(rows, lax.axis_index("gy") * width, width, 1)
    hole_term = jnp.dot(occ_integrals, columns, preferred_element_type=F32)
    return ladder_term, hole_term


def line_of_four(amplitudes, virt_integrals, occ_integrals, occ_irrep, virt_irrep):
    z, y, g = (lax.axis_index(name) for name in ("gx", "gy", "gz"))
    mirrored = z >= 2
    first = (y == 1) != mirrored
    inner = (z == 1) | (z == 2)
    part = amplitudes.shape[0] // 2
    cols = virt_integrals.shape[1]

    def over_gz(value, flip):
        return lax.ppermute(value, "gz", [(i, i ^ flip) for i in range(4)])

    def over_gy(value):
        return lax.ppermute(value, "gy", [(0, 1), (1, 0)])

    def over_gx(packed, pairs):
        return tuple(lax.ppermute(item, "gx", pairs) for item in packed)

    def own_part(start):
        rows = lax.dynamic_slice_in_dim(amplitudes, start, part, 0)
        labels = lax.dynamic_slice_in_dim(occ_irrep, start, part, 0)
        return masked_rows(rows, labels, virt_irrep)

    def pick(condition, one, other):
        return jnp.where(condition, one, other)

    def near(value):
        return value, over_gz(value, 1)

    odd = pick(mirrored, 0, part)
    high, low = own_part(odd), own_part(part - odd)

    y_high = over_gy(high)
    x_high = over_gz(high, 2)
    high_near = near(high)
    y_low = over_gy(low)
    y_high_near = near(y_high)
    yx_high = over_gz(y_high, 2)
    high_far = near(x_high)
    two, zero = pick(first, low, y_low), pick(first, y_low, low)
    x_two = over_gz(two, 2)
    two_near, zero_near = near(two), near(zero)
    y_high_far = near(yx_high)
    two_far = near(x_two)
    x_zero = over_gz(zero, 2)
    zero_far = near(x_zero)

    def times(rows):
        return product(*rows, virt_integrals)

    def choose(condition, one, other):
        return tuple(pick(condition, left, right) for left, right in zip(one, other))

    def send(valued, pairs):
        value, top = valued
        exponent = jnp.ceil(jnp.log2(jnp.maximum(top, 1e-30)))
        body = (value * jnp.exp2(TOP_EXPONENT - exponent)).astype(WIRE)
        tail = jnp.full((EXTRA, cols), exponent, F32).astype(WIRE)
        return lax.ppermute(jnp.concatenate([body, tail], axis=0), "gx", pairs)

    def got(packed):
        exponent = packed[-1, 0].astype(F32)
        return packed[:-EXTRA].astype(F32) * jnp.exp2(exponent - TOP_EXPONENT), jnp.exp2(exponent)

    def plus(one, other):
        return one[0] + other[0], one[1] + other[1]

    next_in, two_in = [(0, 1), (3, 2)], [(0, 2), (3, 1)]
    middle, next_out, two_out = [(1, 2), (2, 1)], [(2, 3), (1, 0)], [(1, 3), (2, 0)]

    p_high_near = times(high_near)
    a0 = send(p_high_near, next_in)
    p_high_far = times(high_far)
    p_y_high_near = times(y_high_near)
    a1 = send(choose(first, p_high_far, p_y_high_near), next_in)
    p_y_high_far = times(y_high_far)
    a2 = send(choose(first, p_y_high_near, p_y_high_far), next_in)
    c_near = send(plus(got(pick(first, a0, a1)), choose(first, p_high_near, p_y_high_near)), two_out)
    p_two_near = times(two_near)
    m_near = send(p_two_near, middle)
    p_two_far = times(two_far)
    e_far = send(p_two_far, two_in)
    c_far = send(plus(got(pick(first, a1, a2)), choose(first, p_high_far, p_y_high_far)), two_out)
    m_far = send(p_two_far, middle)
    a3 = send(choose(first, p_y_high_far, p_high_far), next_in)
    p_zero_far = times(zero_far)
    p_zero_near = times(zero_near)
    o_far = send(p_zero_far, next_out)
    o_near = send(p_zero_near, next_out)
    e_near = send(p_two_near, two_in)

    base_near = pick(inner, pick(first, p_y_high_near[0], p_high_near[0]), p_zero_near[0])
    base_far = pick(inner, pick(first, p_y_high_far[0], p_high_far[0]), p_zero_far[0])

    def total(base, *arrived):
        return functools.reduce(lambda sofar, packed: sofar + got(packed)[0], arrived, base)

    total_far = total(base_far, m_far, o_far, c_far, e_far, a3)
    total_near = total(base_near, m_near, o_near, c_near, pick(first, a2, a0), e_near)

    blocks = [
        total_near[:part],
        over_gz(total_near[part:], 1),
        over_gz(total_far[:part], 2),
        over_gz(total_far[part:], 3),
    ]
    ladder_term = jnp.zeros((part, 4 * cols), F32)
    for flip, block in enumerate(blocks):
        ladder_term = lax.dynamic_update_slice(ladder_term, block, (0, (g ^ flip) * cols))

    def owner(index):
        return pick(mirrored, 3 - index, index)

    held = (
        (owner(pick(first, 3, 1)), high_near + high_far),
        (owner(pick(first, 1, 3)), y_high_near + y_high_far),
        (owner(2), two_near + two_far),
        (owner(0), zero_near + zero_far),
    )
    row_blocks = [block for _, group in held for block in group]
    places = [(g ^ flip) * 4 + place for place, _ in held for flip in range(4)]
    hole_term = hole_product(occ_integrals, row_blocks, places, y)
    return ladder_term, hole_term


def solution(mesh):
    placed = (P(("gz", "gy"), "gx"), P("gx", ("gy", "gz")), P("gz", None), P(("gz", "gy")), P("gx"))
    sizes = tuple(mesh.shape[name] for name in ("gx", "gy", "gz"))
    return jax.shard_map(
        line_of_four if sizes == (4, 2, 4) else whole_sums,
        mesh=mesh,
        in_specs=placed,
        out_specs=(P(("gz", "gx"), "gy"), P("gz", ("gx", "gy"))),
        check_vma=False,
    )
```

```python
import functools

import jax
import jax.numpy as jnp
from jax import lax
from jax.experimental import pallas as pl
from jax.experimental.pallas import tpu as pltpu
from jax.sharding import PartitionSpec as P

F32 = jnp.float32
WIRE = jnp.float16
TOP_EXPONENT = 14.0
EXTRA = 8


def products_kernel(count, part, *refs):
    rows_refs, rest = refs[:2 * count], refs[2 * count:]
    integrals_ref, out_refs, info_refs = rest[0], rest[-2 * count - 3:-count - 3], rest[-count - 3:-3]
    gathered_ref, tops_ref, sems = rest[-3:]
    step, last = pl.program_id(0), pl.num_programs(0) - 1

    @pl.when(step == 0)
    def _():
        copies = [
            pltpu.make_async_copy(rows_ref, gathered_ref.at[pl.ds(index * part, part)], sems.at[index])
            for index, rows_ref in enumerate(rows_refs)
        ]
        for copy in copies:
            copy.start()
        tops_ref[...] = jnp.zeros_like(tops_ref)
        for copy in copies:
            copy.wait()

    value = jnp.dot(gathered_ref[...], integrals_ref[...], preferred_element_type=F32)
    for index, (out_ref, info_ref) in enumerate(zip(out_refs, info_refs)):
        own = value[2 * part * index:2 * part * (index + 1)]
        out_ref[:2 * part] = own
        out_ref[2 * part:] = jnp.zeros((EXTRA, own.shape[1]), F32)
        tops_ref[index] = jnp.maximum(tops_ref[index], jnp.max(jnp.abs(own).reshape(-1, 8, own.shape[1]), axis=0))

        @pl.when(step == last)
        def _():
            top = jnp.maximum(jnp.max(tops_ref[index]), 1e-30)
            exponent = jnp.ceil(jnp.log2(jnp.full((8, info_ref.shape[1]), top, F32)))
            info_ref[:8] = exponent
            info_ref[8:] = jnp.exp2(TOP_EXPONENT - exponent)


def products(pairs, integrals, after=()):
    part, depth = pairs[0][0].shape
    count, cols = len(pairs), integrals.shape[1]
    width = min(cols, 256)
    rows = 2 * part + EXTRA
    anywhere = pl.BlockSpec(memory_space=pl.ANY)
    results = pl.pallas_call(
        functools.partial(products_kernel, count, part),
        grid=(cols // width,),
        in_specs=[anywhere] * (2 * count) + [pl.BlockSpec((depth, width), lambda j: (0, j))] + [anywhere] * len(after),
        out_specs=[pl.BlockSpec((rows, width), lambda j: (0, j))] * count + [pl.BlockSpec((16, cols), lambda j: (0, 0))] * count,
        out_shape=[jax.ShapeDtypeStruct((rows, cols), F32)] * count + [jax.ShapeDtypeStruct((16, cols), F32)] * count,
        scratch_shapes=[
            pltpu.VMEM((2 * count * part, depth), pairs[0][0].dtype),
            pltpu.VMEM((count, 8, width), F32),
            pltpu.SemaphoreType.DMA((2 * count,)),
        ],
        compiler_params=pltpu.CompilerParams(vmem_limit_bytes=56 << 20),
        cost_estimate=pl.CostEstimate(flops=2_000_000_000 * count, bytes_accessed=2_000_000_000 * count // 1000, transcendentals=0),
    )(*[block for pair in pairs for block in pair], integrals, *after)
    return [(result, info[:1], info[8:9]) for result, info in zip(results[:count], results[count:])]


def hole_kernel(count, places_ref, *refs):
    rows_refs, occ_ref = refs[:count], refs[count]
    out_ref, columns_ref = refs[-2:]
    part = rows_refs[0].shape[0]
    for index, rows_ref in enumerate(rows_refs):
        start = pl.multiple_of(places_ref[index] * part, part)
        columns_ref[pl.ds(start, part), :] = rows_ref[...]
    out_ref[...] = jnp.dot(occ_ref[...], columns_ref[...], preferred_element_type=F32)


def hole_product(occ, row_blocks, places, half, after=()):
    part, depth = row_blocks[0].shape
    cols = depth // 2
    width = min(cols, 512)
    steps = cols // width
    return pl.pallas_call(
        functools.partial(hole_kernel, len(row_blocks)),
        grid_spec=pltpu.PrefetchScalarGridSpec(
            num_scalar_prefetch=1,
            grid=(steps,),
            in_specs=[pl.BlockSpec((part, width), lambda j, scalars: (0, scalars[len(row_blocks)] * steps + j))] * len(row_blocks)
            + [pl.BlockSpec(occ.shape, lambda j, scalars: (0, 0))]
            + [pl.BlockSpec(memory_space=pl.ANY)] * len(after),
            out_specs=pl.BlockSpec((occ.shape[0], width), lambda j, scalars: (0, j)),
            scratch_shapes=[pltpu.VMEM((occ.shape[1], width), occ.dtype)],
        ),
        out_shape=jax.ShapeDtypeStruct((occ.shape[0], cols), F32),
        compiler_params=pltpu.CompilerParams(vmem_limit_bytes=56 << 20),
        cost_estimate=pl.CostEstimate(flops=2_000_000_000, bytes_accessed=2_000_000_000 // 1000, transcendentals=0),
    )(jnp.stack([*places, half]).astype(jnp.int32), *row_blocks, occ, *after)


def masked_rows(amplitudes, occ_irrep, virt_irrep):
    keep = occ_irrep[:, None] == virt_irrep[None, :]
    return jnp.where(keep, amplitudes, jnp.zeros_like(amplitudes))


def whole_sums(amplitudes, virt_integrals, occ_integrals, occ_irrep, virt_irrep):
    masked = masked_rows(amplitudes, occ_irrep, virt_irrep)
    rows = lax.all_gather(masked, ("gz", "gy"), axis=0, tiled=True)
    partial = jnp.dot(rows, virt_integrals, preferred_element_type=F32)
    nx, nz = lax.axis_size("gx"), lax.axis_size("gz")
    by_owner = partial.reshape(nz, nx, -1, partial.shape[1]).swapaxes(0, 1)
    mine = lax.psum_scatter(by_owner, "gx", scatter_dimension=0, tiled=True)
    ladder_term = lax.all_to_all(mine[0], "gz", split_axis=0, concat_axis=2, tiled=True)[0]
    width = rows.shape[1] // lax.axis_size("gy")
    columns = lax.dynamic_slice_in_dim(rows, lax.axis_index("gy") * width, width, 1)
    hole_term = jnp.dot(occ_integrals, columns, preferred_element_type=F32)
    return ladder_term, hole_term


def line_of_four(amplitudes, virt_integrals, occ_integrals, occ_irrep, virt_irrep):
    z, y, g = (lax.axis_index(name) for name in ("gx", "gy", "gz"))
    mirrored = z >= 2
    first = (y == 1) != mirrored
    inner = (z == 1) | (z == 2)
    part = amplitudes.shape[0] // 2
    cols = virt_integrals.shape[1]

    def over_gz(value, flip):
        return lax.ppermute(value, "gz", [(i, i ^ flip) for i in range(4)])

    def over_gy(value):
        return lax.ppermute(value, "gy", [(0, 1), (1, 0)])

    def over_gx(packed, pairs):
        return tuple(lax.ppermute(item, "gx", pairs) for item in packed)

    def own_part(start):
        rows = lax.dynamic_slice_in_dim(amplitudes, start, part, 0)
        labels = lax.dynamic_slice_in_dim(occ_irrep, start, part, 0)
        return masked_rows(rows, labels, virt_irrep)

    def pick(condition, one, other):
        return jnp.where(condition, one, other)

    def near(value):
        return value, over_gz(value, 1)

    odd = pick(mirrored, 0, part)
    high, low = own_part(odd), own_part(part - odd)

    y_high = over_gy(high)
    x_high = over_gz(high, 2)
    high_near = near(high)
    y_low = over_gy(low)
    y_high_near = near(y_high)
    yx_high = over_gz(y_high, 2)
    high_far = near(x_high)
    two, zero = pick(first, low, y_low), pick(first, y_low, low)
    x_two = over_gz(two, 2)
    two_near, zero_near = near(two), near(zero)
    y_high_far = near(yx_high)
    two_far = near(x_two)
    x_zero = over_gz(zero, 2)
    zero_far = near(x_zero)

    def choose(condition, one, other):
        return tuple(pick(condition, left, right) for left, right in zip(one, other))

    spare = lax.broadcasted_iota(jnp.int32, (2 * part + EXTRA, 1), 0) >= 2 * part

    def send(scaled, pairs):
        value, exponent, scale = scaled
        return lax.ppermute(jnp.where(spare, exponent, value * scale).astype(WIRE), "gx", pairs)

    def exponent_of(packed):
        return packed[2 * part:2 * part + 1].astype(F32)

    def got(packed):
        exponent = exponent_of(packed)
        return packed.astype(F32) * jnp.exp2(exponent - TOP_EXPONENT), exponent

    def plus(arrived, own):
        value, exponent = got(arrived)
        exponent = jnp.maximum(exponent, own[1]) + 1.0
        return value + own[0], exponent, jnp.exp2(TOP_EXPONENT - exponent)

    next_in, two_in = [(0, 1), (3, 2)], [(0, 2), (3, 1)]
    middle, next_out, two_out = [(1, 2), (2, 1)], [(2, 3), (1, 0)], [(1, 3), (2, 0)]

    (p_high_near,) = products([high_near], virt_integrals)
    a0 = send(p_high_near, next_in)
    p_high_far, p_y_high_near = products([high_far, y_high_near], virt_integrals)
    a1 = send(choose(first, p_high_far, p_y_high_near), next_in)
    p_y_high_far, p_two_near = products([y_high_far, two_near], virt_integrals, [exponent_of(a0)])
    a2 = send(choose(first, p_y_high_near, p_y_high_far), next_in)
    m_near = send(p_two_near, middle)
    c_near = send(plus(pick(first, a0, a1), choose(first, p_high_near, p_y_high_near)), two_out)
    (p_two_far,) = products([two_far], virt_integrals, [exponent_of(a1)])
    e_far = send(p_two_far, two_in)
    c_far = send(plus(pick(first, a1, a2), choose(first, p_high_far, p_y_high_far)), two_out)
    m_far = send(p_two_far, middle)
    a3 = send(choose(first, p_y_high_far, p_high_far), next_in)
    p_zero_far, p_zero_near = products([zero_far, zero_near], virt_integrals, [exponent_of(a2), exponent_of(c_near), exponent_of(m_near)])
    o_far = send(p_zero_far, next_out)
    o_near = send(p_zero_near, next_out)
    e_near = send(p_two_near, two_in)

    base_near = pick(inner, pick(first, p_y_high_near[0], p_high_near[0]), p_zero_near[0])
    base_far = pick(inner, pick(first, p_y_high_far[0], p_high_far[0]), p_zero_far[0])

    def total(base, *arrived):
        return functools.reduce(lambda sofar, packed: sofar + got(packed)[0], arrived, base)

    total_far = total(base_far, m_far, o_far, c_far, e_far, a3)
    total_near = total(base_near, m_near, o_near, c_near, pick(first, a2, a0), e_near)

    blocks = [
        total_near[:part],
        over_gz(total_near[part:2 * part], 1),
        over_gz(total_far[:part], 2),
        over_gz(total_far[part:2 * part], 3),
    ]
    ladder_term = jnp.zeros((part, 4 * cols), F32)
    for flip, block in enumerate(blocks):
        ladder_term = lax.dynamic_update_slice(ladder_term, block, (0, (g ^ flip) * cols))

    def owner(index):
        return pick(mirrored, 3 - index, index)

    held = (
        (owner(pick(first, 3, 1)), high_near + high_far),
        (owner(pick(first, 1, 3)), y_high_near + y_high_far),
        (owner(2), two_near + two_far),
        (owner(0), zero_near + zero_far),
    )
    row_blocks = [block for _, group in held for block in group]
    places = [(g ^ flip) * 4 + place for place, _ in held for flip in range(4)]
    hole_term = hole_product(occ_integrals, row_blocks, places, y, [exponent_of(e_far), exponent_of(c_far), exponent_of(m_far)])
    return ladder_term, hole_term


def solution(mesh):
    placed = (P(("gz", "gy"), "gx"), P("gx", ("gy", "gz")), P("gz", None), P(("gz", "gy")), P("gx"))
    sizes = tuple(mesh.shape[name] for name in ("gx", "gy", "gz"))
    return jax.shard_map(
        line_of_four if sizes == (4, 2, 4) else whole_sums,
        mesh=mesh,
        in_specs=placed,
        out_specs=(P(("gz", "gx"), "gy"), P("gz", ("gx", "gy"))),
        check_vma=False,
    )
```

```python
import functools

import jax
import jax.numpy as jnp
from jax import lax
from jax.experimental import pallas as pl
from jax.experimental.pallas import tpu as pltpu
from jax.sharding import PartitionSpec as P

F32 = jnp.float32
WIRE = jnp.float16
TOP_EXPONENT = 14.0
EXTRA = 8


def hole_kernel(count, places_ref, *refs):
    rows_refs, occ_ref = refs[:count], refs[count]
    out_ref, columns_ref = refs[-2:]
    part = rows_refs[0].shape[0]
    for index, rows_ref in enumerate(rows_refs):
        start = pl.multiple_of(places_ref[index] * part, part)
        columns_ref[pl.ds(start, part), :] = rows_ref[...]
    out_ref[...] = jnp.dot(occ_ref[...], columns_ref[...], preferred_element_type=F32)


def hole_product(occ, row_blocks, places, half):
    part, depth = row_blocks[0].shape
    cols = depth // 2
    width = min(cols, 512)
    steps = cols // width
    return pl.pallas_call(
        functools.partial(hole_kernel, len(row_blocks)),
        grid_spec=pltpu.PrefetchScalarGridSpec(
            num_scalar_prefetch=1,
            grid=(steps,),
            in_specs=[pl.BlockSpec((part, width), lambda j, scalars: (0, scalars[len(row_blocks)] * steps + j))] * len(row_blocks)
            + [pl.BlockSpec(occ.shape, lambda j, scalars: (0, 0))],
            out_specs=pl.BlockSpec((occ.shape[0], width), lambda j, scalars: (0, j)),
            scratch_shapes=[pltpu.VMEM((occ.shape[1], width), occ.dtype)],
        ),
        out_shape=jax.ShapeDtypeStruct((occ.shape[0], cols), F32),
        compiler_params=pltpu.CompilerParams(vmem_limit_bytes=32 << 20),
        cost_estimate=pl.CostEstimate(flops=2_000_000_000, bytes_accessed=2_000_000_000 // 1000, transcendentals=0),
    )(jnp.stack([*places, half]).astype(jnp.int32), *row_blocks, occ)


def masked_rows(amplitudes, occ_irrep, virt_irrep):
    keep = occ_irrep[:, None] == virt_irrep[None, :]
    return jnp.where(keep, amplitudes, jnp.zeros_like(amplitudes))


def whole_sums(amplitudes, virt_integrals, occ_integrals, occ_irrep, virt_irrep):
    masked = masked_rows(amplitudes, occ_irrep, virt_irrep)
    rows = lax.all_gather(masked, ("gz", "gy"), axis=0, tiled=True)
    partial = jnp.dot(rows, virt_integrals, preferred_element_type=F32)
    nx, nz = lax.axis_size("gx"), lax.axis_size("gz")
    by_owner = partial.reshape(nz, nx, -1, partial.shape[1]).swapaxes(0, 1)
    mine = lax.psum_scatter(by_owner, "gx", scatter_dimension=0, tiled=True)
    ladder_term = lax.all_to_all(mine[0], "gz", split_axis=0, concat_axis=2, tiled=True)[0]
    width = rows.shape[1] // lax.axis_size("gy")
    columns = lax.dynamic_slice_in_dim(rows, lax.axis_index("gy") * width, width, 1)
    hole_term = jnp.dot(occ_integrals, columns, preferred_element_type=F32)
    return ladder_term, hole_term


def line_of_four(amplitudes, virt_integrals, occ_integrals, occ_irrep, virt_irrep):
    z, y, g = (lax.axis_index(name) for name in ("gx", "gy", "gz"))
    mirrored = z >= 2
    first = (y == 1) != mirrored
    inner = (z == 1) | (z == 2)
    part = amplitudes.shape[0] // 2
    cols = virt_integrals.shape[1]

    def over_gz(value, flip):
        return lax.ppermute(value, "gz", [(i, i ^ flip) for i in range(4)])

    def over_gy(value):
        return lax.ppermute(value, "gy", [(0, 1), (1, 0)])

    def over_gx(packed, pairs):
        return tuple(lax.ppermute(item, "gx", pairs) for item in packed)

    def own_part(start):
        rows = lax.dynamic_slice_in_dim(amplitudes, start, part, 0)
        labels = lax.dynamic_slice_in_dim(occ_irrep, start, part, 0)
        return masked_rows(rows, labels, virt_irrep)

    def pick(condition, one, other):
        return jnp.where(condition, one, other)

    spare = lax.broadcasted_iota(jnp.int32, (2 * part + EXTRA, 1), 0) >= 2 * part
    blank = jnp.zeros((EXTRA, amplitudes.shape[1]), amplitudes.dtype)
    depth = virt_integrals.shape[0]

    def stage(work):
        skipped = jax.tree.map(lambda leaf: jnp.zeros(leaf.shape, leaf.dtype), jax.eval_shape(work))
        return lax.cond(z < 4, work, lambda: skipped)

    def largest(value):
        return jnp.max(jnp.abs(value)).astype(F32)

    def product(one, other, integral_top):
        rows = jnp.concatenate([one, other, blank], axis=0)
        exponent = jnp.ceil(jnp.log2(jnp.maximum(largest(rows) * integral_top * depth, 1e-30)))
        return jnp.dot(rows, virt_integrals, preferred_element_type=F32), exponent

    def choose(condition, one, other):
        return tuple(pick(condition, left, right) for left, right in zip(one, other))

    def pack(value, exponent):
        return jnp.where(spare, exponent, value * jnp.exp2(TOP_EXPONENT - exponent)).astype(WIRE)

    def got(packed):
        exponent = packed[2 * part:2 * part + 1].astype(F32)
        return packed.astype(F32) * jnp.exp2(exponent - TOP_EXPONENT), exponent

    def plus(packed, own):
        value, exponent = got(packed)
        return pack(value + own[0], jnp.maximum(exponent, own[1]) + 1.0)

    def inward(packed):
        return lax.ppermute(packed, "gx", [(0, 1), (3, 2)])

    def across(packed):
        return lax.ppermute(packed, "gx", [(1, 2), (2, 1)])

    def outward(packed):
        return lax.ppermute(packed, "gx", [(2, 3), (1, 0)])

    def sibling(value):
        return over_gz(value, 1)

    odd = pick(mirrored, 0, part)
    high, low = own_part(odd), own_part(part - odd)

    def work0():
        x_high, y_high, s_high = over_gz(high, 2), over_gy(high), sibling(high)
        top = largest(virt_integrals)
        near = product(high, s_high, top)
        return x_high, y_high, s_high, top, near, pack(*near)

    x_high, y_high, s_high, top, q_high_near, p0 = stage(work0)

    def work1():
        a0, yx_high, y_low = inward(p0), over_gz(y_high, 2), over_gy(low)
        sx_high, sy_high = sibling(x_high), sibling(y_high)
        q_high_far, q_y_high_near = product(x_high, sx_high, top), product(y_high, sy_high, top)
        return a0, yx_high, y_low, sx_high, sy_high, q_high_far, q_y_high_near, pack(*choose(first, q_high_far, q_y_high_near))

    a0, yx_high, y_low, sx_high, sy_high, q_high_far, q_y_high_near, p1 = stage(work1)
    two, zero = pick(first, low, y_low), pick(first, y_low, low)

    def work2():
        a1, x_two, syx_high, s_two = inward(p1), over_gz(two, 2), sibling(yx_high), sibling(two)
        q_y_high_far, q_two_near = product(yx_high, syx_high, top), product(two, s_two, top)
        return a1, x_two, syx_high, s_two, q_y_high_far, q_two_near, pack(*choose(first, q_y_high_near, q_y_high_far))

    a1, x_two, syx_high, s_two, q_y_high_far, q_two_near, p2 = stage(work2)

    def work3():
        b0 = across(plus(pick(first, a0, a1), choose(first, q_high_near, q_y_high_near)))
        a2, x_zero, sx_two, s_zero = inward(p2), over_gz(zero, 2), sibling(x_two), sibling(zero)
        q_two_far, q_zero_near = product(x_two, sx_two, top), product(zero, s_zero, top)
        return b0, a2, x_zero, sx_two, s_zero, q_two_far, q_zero_near, pack(*q_two_far)

    b0, a2, x_zero, sx_two, s_zero, q_two_far, q_zero_near, p3 = stage(work3)

    def work4():
        a3 = inward(p3)
        b1 = across(plus(pick(first, a1, a2), choose(first, q_high_far, q_y_high_far)))
        c0 = outward(plus(b0, q_zero_near))
        sx_zero = sibling(x_zero)
        return a3, b1, c0, sx_zero, product(x_zero, sx_zero, top), pack(*choose(first, q_y_high_far, q_high_far))

    a3, b1, c0, sx_zero, q_zero_far, p4 = stage(work4)

    def owner(index):
        return pick(mirrored, 3 - index, index)

    held = (
        (owner(pick(first, 3, 1)), (high, s_high, x_high, sx_high)),
        (owner(pick(first, 1, 3)), (y_high, sy_high, yx_high, syx_high)),
        (owner(2), (two, s_two, x_two, sx_two)),
        (owner(0), (zero, s_zero, x_zero, sx_zero)),
    )
    row_blocks = [block for _, group in held for block in group]
    places = [(g ^ flip) * 4 + place for place, _ in held for flip in range(4)]

    def total(base, *arrived):
        return functools.reduce(lambda sofar, packed: sofar + got(packed)[0], arrived, base)

    def work5():
        a4, b2, c1 = inward(p4), across(plus(a3, q_two_far)), outward(plus(b1, q_zero_far))
        hole_term = hole_product(occ_integrals, row_blocks, places, y)
        total_far = total(pick(inner, pick(first, q_y_high_far[0], q_high_far[0]), q_zero_far[0]), a4, b2, c1)
        return total_far[:part], total_far[part:2 * part], hole_term, pack(*q_two_near)

    far_one, far_two, hole_term, p5 = stage(work5)

    def work6():
        return inward(p5), over_gz(far_one, 2)

    a5, block_two = stage(work6)

    def work7():
        b3, block_three = across(plus(a5, q_two_near)), over_gz(far_two, 3)
        base = pick(inner, pick(first, q_y_high_near[0], q_high_near[0]), q_zero_near[0])
        total_near = total(base, c0, pick(first, a2, a0), b3)
        return block_three, total_near[:part], sibling(total_near[part:2 * part])

    block_three, block_zero, block_one = stage(work7)

    ladder_term = jnp.zeros((part, 4 * cols), F32)
    for flip, block in enumerate((block_zero, block_one, block_two, block_three)):
        ladder_term = lax.dynamic_update_slice(ladder_term, block, (0, (g ^ flip) * cols))
    return ladder_term, hole_term


def solution(mesh):
    placed = (P(("gz", "gy"), "gx"), P("gx", ("gy", "gz")), P("gz", None), P(("gz", "gy")), P("gx"))
    sizes = tuple(mesh.shape[name] for name in ("gx", "gy", "gz"))
    return jax.shard_map(
        line_of_four if sizes == (4, 2, 4) else whole_sums,
        mesh=mesh,
        in_specs=placed,
        out_specs=(P(("gz", "gx"), "gy"), P("gz", ("gx", "gy"))),
        check_vma=False,
    )
```

```python
import functools

import jax
import jax.numpy as jnp
from jax import lax
from jax.experimental import pallas as pl
from jax.experimental.pallas import tpu as pltpu
from jax.sharding import PartitionSpec as P

F32 = jnp.float32
WIRE = jnp.float16
TOP_EXPONENT = 14.0
EXTRA = 8


def products_kernel(count, order_ref, *refs):
    rows_refs, integrals_ref = refs[:2 * count], refs[2 * count]
    out_refs, info_refs = refs[2 * count + 1:3 * count + 1], refs[3 * count + 1:]
    rows, cols = 2 * rows_refs[0].shape[0], integrals_ref.shape[1]
    width = min(cols, 512)
    step, last = pl.program_id(0), pl.num_programs(0) - 1

    @pl.when(step == 0)
    def _():
        for out_ref in out_refs:
            out_ref[...] = jnp.zeros_like(out_ref)

    blocks = [rows_ref[...] for rows_ref in rows_refs]
    if count == 2:
        swapped = order_ref[0] == 1
        blocks = [jnp.where(swapped, blocks[(i + 2) % 4], blocks[i]) for i in range(4)]
    gathered = jnp.concatenate(blocks, axis=0)
    for start in range(0, cols, width):
        value = jnp.dot(gathered, integrals_ref[:, start:start + width], preferred_element_type=F32)
        for index, out_ref in enumerate(out_refs):
            out_ref[:rows, start:start + width] += value[rows * index:rows * (index + 1)]

    @pl.when(step == last)
    def _():
        for out_ref, info_ref in zip(out_refs, info_refs):
            top = jnp.zeros((8, width), F32)
            for start in range(0, cols, width):
                size = jnp.abs(out_ref[:rows, start:start + width]).reshape(-1, 8, width)
                top = jnp.maximum(top, jnp.max(size, axis=0))
            largest = jnp.maximum(jnp.max(top), 1e-30)
            exponent = jnp.ceil(jnp.log2(jnp.full((8, cols), largest, F32)))
            info_ref[:8] = exponent
            info_ref[8:] = jnp.exp2(TOP_EXPONENT - exponent)


def products(pairs, integrals, swapped):
    part, depth = pairs[0][0].shape
    count, cols = len(pairs), integrals.shape[1]
    block = min(depth, 512)
    rows = 2 * part + EXTRA
    results = pl.pallas_call(
        functools.partial(products_kernel, count),
        grid_spec=pltpu.PrefetchScalarGridSpec(
            num_scalar_prefetch=1,
            grid=(depth // block,),
            in_specs=[pl.BlockSpec((part, block), lambda k, _: (0, k))] * (2 * count)
            + [pl.BlockSpec((block, cols), lambda k, _: (k, 0))],
            out_specs=[pl.BlockSpec((rows, cols), lambda k, _: (0, 0))] * count
            + [pl.BlockSpec((16, cols), lambda k, _: (0, 0))] * count,
        ),
        out_shape=[jax.ShapeDtypeStruct((rows, cols), F32)] * count + [jax.ShapeDtypeStruct((16, cols), F32)] * count,
        compiler_params=pltpu.CompilerParams(vmem_limit_bytes=40 << 20),
        cost_estimate=pl.CostEstimate(flops=2_000_000_000, bytes_accessed=2_000_000, transcendentals=0),
    )(swapped.astype(jnp.int32).reshape(1), *[block for pair in pairs for block in pair], integrals)
    return [(result, info[:1], info[8:9]) for result, info in zip(results[:count], results[count:])]


def hole_kernel(count, places_ref, *refs):
    rows_refs, occ_ref = refs[:count], refs[count]
    out_ref, columns_ref = refs[-2:]
    part = rows_refs[0].shape[0]
    for index, rows_ref in enumerate(rows_refs):
        start = pl.multiple_of(places_ref[index] * part, part)
        columns_ref[pl.ds(start, part), :] = rows_ref[...]
    out_ref[...] = jnp.dot(occ_ref[...], columns_ref[...], preferred_element_type=F32)


def hole_product(occ, row_blocks, places, half):
    part, depth = row_blocks[0].shape
    cols = depth // 2
    width = min(cols, 512)
    steps = cols // width
    return pl.pallas_call(
        functools.partial(hole_kernel, len(row_blocks)),
        grid_spec=pltpu.PrefetchScalarGridSpec(
            num_scalar_prefetch=1,
            grid=(steps,),
            in_specs=[pl.BlockSpec((part, width), lambda j, scalars: (0, scalars[len(row_blocks)] * steps + j))] * len(row_blocks)
            + [pl.BlockSpec(occ.shape, lambda j, scalars: (0, 0))],
            out_specs=pl.BlockSpec((occ.shape[0], width), lambda j, scalars: (0, j)),
            scratch_shapes=[pltpu.VMEM((occ.shape[1], width), occ.dtype)],
        ),
        out_shape=jax.ShapeDtypeStruct((occ.shape[0], cols), F32),
        compiler_params=pltpu.CompilerParams(vmem_limit_bytes=32 << 20),
        cost_estimate=pl.CostEstimate(flops=2_000_000_000, bytes_accessed=2_000_000_000 // 1000, transcendentals=0),
    )(jnp.stack([*places, half]).astype(jnp.int32), *row_blocks, occ)


def masked_rows(amplitudes, occ_irrep, virt_irrep):
    keep = occ_irrep[:, None] == virt_irrep[None, :]
    return jnp.where(keep, amplitudes, jnp.zeros_like(amplitudes))


def whole_sums(amplitudes, virt_integrals, occ_integrals, occ_irrep, virt_irrep):
    masked = masked_rows(amplitudes, occ_irrep, virt_irrep)
    rows = lax.all_gather(masked, ("gz", "gy"), axis=0, tiled=True)
    partial = jnp.dot(rows, virt_integrals, preferred_element_type=F32)
    nx, nz = lax.axis_size("gx"), lax.axis_size("gz")
    by_owner = partial.reshape(nz, nx, -1, partial.shape[1]).swapaxes(0, 1)
    mine = lax.psum_scatter(by_owner, "gx", scatter_dimension=0, tiled=True)
    ladder_term = lax.all_to_all(mine[0], "gz", split_axis=0, concat_axis=2, tiled=True)[0]
    width = rows.shape[1] // lax.axis_size("gy")
    columns = lax.dynamic_slice_in_dim(rows, lax.axis_index("gy") * width, width, 1)
    hole_term = jnp.dot(occ_integrals, columns, preferred_element_type=F32)
    return ladder_term, hole_term


def line_of_four(amplitudes, virt_integrals, occ_integrals, occ_irrep, virt_irrep):
    z, y, g = (lax.axis_index(name) for name in ("gx", "gy", "gz"))
    mirrored = z >= 2
    first = (y == 1) != mirrored
    inner = (z == 1) | (z == 2)
    part = amplitudes.shape[0] // 2
    cols = virt_integrals.shape[1]

    def over_gz(value, flip):
        return lax.ppermute(value, "gz", [(i, i ^ flip) for i in range(4)])

    def over_gy(value):
        return lax.ppermute(value, "gy", [(0, 1), (1, 0)])

    def over_gx(packed, pairs):
        return tuple(lax.ppermute(item, "gx", pairs) for item in packed)

    def own_part(start):
        rows = lax.dynamic_slice_in_dim(amplitudes, start, part, 0)
        labels = lax.dynamic_slice_in_dim(occ_irrep, start, part, 0)
        return masked_rows(rows, labels, virt_irrep)

    def pick(condition, one, other):
        return jnp.where(condition, one, other)

    spare = lax.broadcasted_iota(jnp.int32, (2 * part + EXTRA, 1), 0) >= 2 * part
    def stage(work):
        skipped = jax.tree.map(lambda leaf: jnp.zeros(leaf.shape, leaf.dtype), jax.eval_shape(work))
        return lax.cond(z < 4, work, lambda: skipped)

    def times(*pairs, swapped=jnp.bool_(False)):
        return products(pairs, virt_integrals, swapped)

    def choose(condition, one, other):
        return tuple(pick(condition, left, right) for left, right in zip(one, other))

    def pack(value, exponent, scale):
        return jnp.where(spare, exponent, value * scale).astype(WIRE)

    def got(packed):
        exponent = packed[2 * part:2 * part + 1].astype(F32)
        return packed.astype(F32) * jnp.exp2(exponent - TOP_EXPONENT), exponent

    def plus(packed, own):
        value, exponent = got(packed)
        exponent = jnp.maximum(exponent, own[1]) + 1.0
        return pack(value + own[0], exponent, jnp.exp2(TOP_EXPONENT - exponent))

    def inward(packed):
        return lax.ppermute(packed, "gx", [(0, 1), (3, 2)])

    def across(packed):
        return lax.ppermute(packed, "gx", [(1, 2), (2, 1)])

    def outward(packed):
        return lax.ppermute(packed, "gx", [(2, 3), (1, 0)])

    def sibling(value):
        return over_gz(value, 1)

    odd = pick(mirrored, 0, part)
    high, low = own_part(odd), own_part(part - odd)

    def work0():
        x_high, y_high, s_high = over_gz(high, 2), over_gy(high), sibling(high)
        (near,) = times((high, s_high))
        return x_high, y_high, s_high, near, pack(*near)

    x_high, y_high, s_high, q_high_near, p0 = stage(work0)

    def work1():
        a0, yx_high, y_low = inward(p0), over_gz(y_high, 2), over_gy(low)
        sx_high, sy_high = sibling(x_high), sibling(y_high)
        urgent, rest = times((x_high, sx_high), (y_high, sy_high), swapped=~first)
        return a0, yx_high, y_low, sx_high, sy_high, urgent, rest, pack(*urgent)

    a0, yx_high, y_low, sx_high, sy_high, q_urgent, q_rest, p1 = stage(work1)
    two, zero = pick(first, low, y_low), pick(first, y_low, low)

    def work2():
        a1, x_two, syx_high, s_two = inward(p1), over_gz(two, 2), sibling(yx_high), sibling(two)
        y_high_far, two_near = times((yx_high, syx_high), (two, s_two))
        return a1, x_two, syx_high, s_two, y_high_far, two_near, pack(*choose(first, q_rest, y_high_far))

    a1, x_two, syx_high, s_two, q_y_high_far, q_two_near, p2 = stage(work2)

    def work3():
        b0 = across(plus(pick(first, a0, a1), choose(first, q_high_near, q_urgent)))
        a2, x_zero, sx_two, s_zero = inward(p2), over_gz(zero, 2), sibling(x_two), sibling(zero)
        two_far, zero_near = times((x_two, sx_two), (zero, s_zero))
        return b0, a2, x_zero, sx_two, s_zero, two_far, zero_near, pack(*two_far)

    b0, a2, x_zero, sx_two, s_zero, q_two_far, q_zero_near, p3 = stage(work3)

    def work4():
        a3 = inward(p3)
        b1 = across(plus(pick(first, a1, a2), choose(first, q_urgent, q_y_high_far)))
        c0 = outward(plus(b0, q_zero_near))
        sx_zero = sibling(x_zero)
        (zero_far,) = times((x_zero, sx_zero))
        return a3, b1, c0, sx_zero, zero_far, pack(*choose(first, q_y_high_far, q_rest))

    a3, b1, c0, sx_zero, q_zero_far, p4 = stage(work4)

    def owner(index):
        return pick(mirrored, 3 - index, index)

    held = (
        (owner(pick(first, 3, 1)), (high, s_high, x_high, sx_high)),
        (owner(pick(first, 1, 3)), (y_high, sy_high, yx_high, syx_high)),
        (owner(2), (two, s_two, x_two, sx_two)),
        (owner(0), (zero, s_zero, x_zero, sx_zero)),
    )
    row_blocks = [block for _, group in held for block in group]
    places = [(g ^ flip) * 4 + place for place, _ in held for flip in range(4)]

    def total(base, *arrived):
        return functools.reduce(lambda sofar, packed: sofar + got(packed)[0], arrived, base)

    def work5():
        a4, b2, c1 = inward(p4), across(plus(a3, q_two_far)), outward(plus(b1, q_zero_far))
        total_far = total(pick(inner, pick(first, q_y_high_far[0], q_rest[0]), q_zero_far[0]), a4, b2, c1)
        return total_far[:part], total_far[part:2 * part], pack(*q_two_near)

    far_one, far_two, p5 = stage(work5)

    def work6():
        a5, block_two = inward(p5), over_gz(far_one, 2)
        base = pick(inner, pick(first, q_rest[0], q_high_near[0]), q_zero_near[0])
        hole_term = hole_product(occ_integrals, row_blocks, places, y)
        return a5, block_two, total(base, c0, pick(first, a2, a0)), hole_term

    a5, block_two, almost_near, hole_term = stage(work6)

    b3, block_three = across(plus(a5, q_two_near)), over_gz(far_two, 3)
    total_near = total(almost_near, b3)
    ladder_term = jnp.zeros((part, 4 * cols), F32)
    for flip, block in ((2, block_two), (0, total_near[:part]), (1, sibling(total_near[part:2 * part])), (3, block_three)):
        ladder_term = lax.dynamic_update_slice(ladder_term, block, (0, (g ^ flip) * cols))
    return ladder_term, hole_term


def solution(mesh):
    placed = (P(("gz", "gy"), "gx"), P("gx", ("gy", "gz")), P("gz", None), P(("gz", "gy")), P("gx"))
    sizes = tuple(mesh.shape[name] for name in ("gx", "gy", "gz"))
    return jax.shard_map(
        line_of_four if sizes == (4, 2, 4) else whole_sums,
        mesh=mesh,
        in_specs=placed,
        out_specs=(P(("gz", "gx"), "gy"), P("gz", ("gx", "gy"))),
        check_vma=False,
    )
```

```python
import functools

import jax
import jax.numpy as jnp
from jax import lax
from jax.experimental import pallas as pl
from jax.experimental.pallas import tpu as pltpu
from jax.sharding import PartitionSpec as P

F32 = jnp.float32
CODE = jnp.int16
TAIL = 16
FINE = 64.0
LOG_TOP = 29.9
SMALLEST = 1e-27


def coded(value):
    largest = jnp.maximum(jnp.max(jnp.abs(value)), SMALLEST)
    level = jnp.ceil(jnp.log2(jnp.full((TAIL, value.shape[1]), largest, F32)) * FINE)
    factor = jnp.exp2(LOG_TOP - level[:1] * (1.0 / FINE))
    size = (jnp.sqrt(jnp.abs(value) * factor) + 0.5).astype(jnp.int32)
    return jnp.where(value < 0.0, -size, size).astype(CODE), level.astype(jnp.int32).astype(CODE)


def decoded(ref, rows):
    code = ref[:rows, :].astype(jnp.int32).astype(F32)
    level = ref[rows:, :].astype(jnp.int32).astype(F32)[:1]
    return code * jnp.abs(code) * jnp.exp2(level * (1.0 / FINE) - LOG_TOP)


def write_coded(ref, value, start, width):
    rows = value.shape[0]
    code, level = coded(value)
    ref[:rows, start:start + width] = code
    ref[rows:, start:start + width] = level


def products_kernel(count, order_ref, *refs):
    rows_refs, integrals_ref = refs[:2 * count], refs[2 * count]
    out_refs, code_refs = refs[2 * count + 1:3 * count + 1], refs[3 * count + 1:]
    rows, cols = 2 * rows_refs[0].shape[0], integrals_ref.shape[1]
    width = min(cols, 512)
    step, last = pl.program_id(0), pl.num_programs(0) - 1

    @pl.when(step == 0)
    def _():
        for out_ref in out_refs:
            out_ref[...] = jnp.zeros_like(out_ref)

    blocks = [rows_ref[...] for rows_ref in rows_refs]
    if count == 2:
        swapped = order_ref[0] == 1
        blocks = [jnp.where(swapped, blocks[(i + 2) % 4], blocks[i]) for i in range(4)]
    gathered = jnp.concatenate(blocks, axis=0)
    for start in range(0, cols, width):
        value = jnp.dot(gathered, integrals_ref[:, start:start + width], preferred_element_type=F32)
        for index, out_ref in enumerate(out_refs):
            out_ref[:, start:start + width] += value[rows * index:rows * (index + 1)]

    @pl.when(step == last)
    def _():
        for out_ref, code_ref in zip(out_refs, code_refs):
            for start in range(0, cols, width):
                write_coded(code_ref, out_ref[:, start:start + width], start, width)


def products(pairs, integrals, swapped):
    part, depth = pairs[0][0].shape
    count, cols = len(pairs), integrals.shape[1]
    block = min(depth, 512)
    rows = 2 * part
    results = pl.pallas_call(
        functools.partial(products_kernel, count),
        grid_spec=pltpu.PrefetchScalarGridSpec(
            num_scalar_prefetch=1,
            grid=(depth // block,),
            in_specs=[pl.BlockSpec((part, block), lambda k, _: (0, k))] * (2 * count)
            + [pl.BlockSpec((block, cols), lambda k, _: (k, 0))],
            out_specs=[pl.BlockSpec((rows, cols), lambda k, _: (0, 0))] * count
            + [pl.BlockSpec((rows + TAIL, cols), lambda k, _: (0, 0))] * count,
        ),
        out_shape=[jax.ShapeDtypeStruct((rows, cols), F32)] * count
        + [jax.ShapeDtypeStruct((rows + TAIL, cols), CODE)] * count,
        compiler_params=pltpu.CompilerParams(vmem_limit_bytes=40 << 20),
        cost_estimate=pl.CostEstimate(flops=2_000_000_000, bytes_accessed=2_000_000, transcendentals=0),
    )(swapped.astype(jnp.int32).reshape(1), *[block for pair in pairs for block in pair], integrals)
    return list(zip(results[:count], results[count:]))


def sums_kernel(kind, bases, choices, arrivals, flags_ref, *refs):
    base_refs, refs = refs[:bases], refs[bases:]
    choice_refs, refs = refs[:choices], refs[choices:]
    arrival_refs, out_refs, total_ref = refs[:arrivals], refs[arrivals:-1], refs[-1]
    rows, width = total_ref.shape
    for index, base_ref in enumerate(base_refs):

        @pl.when(flags_ref[0] == index)
        def _():
            total_ref[...] = base_ref[...]

    for index, choice_ref in enumerate(choice_refs):

        @pl.when(flags_ref[1] == index)
        def _():
            total_ref[...] += decoded(choice_ref, rows)

    total = total_ref[...]
    for arrival_ref in arrival_refs:
        total += decoded(arrival_ref, rows)
    each = rows // len(out_refs)
    for index, out_ref in enumerate(out_refs):
        own = total[each * index:each * (index + 1)]
        if kind == "plain":
            out_ref[...] = own
        else:
            write_coded(out_ref, own, 0, width)


def sums(kind, outs, bases, base, choices, choice, arrivals):
    rows, cols = bases[0].shape
    width = min(cols, 512)
    each = rows // outs + (0 if kind == "plain" else TAIL)
    return pl.pallas_call(
        functools.partial(sums_kernel, kind, len(bases), len(choices), len(arrivals)),
        grid_spec=pltpu.PrefetchScalarGridSpec(
            num_scalar_prefetch=1,
            grid=(cols // width,),
            in_specs=[pl.BlockSpec((rows, width), lambda j, _: (0, j))] * len(bases)
            + [pl.BlockSpec((rows + TAIL, width), lambda j, _: (0, j))] * (len(choices) + len(arrivals)),
            out_specs=[pl.BlockSpec((each, width), lambda j, _: (0, j))] * outs,
            scratch_shapes=[pltpu.VMEM((rows, width), F32)],
        ),
        out_shape=[jax.ShapeDtypeStruct((each, cols), F32 if kind == "plain" else CODE)] * outs,
        compiler_params=pltpu.CompilerParams(vmem_limit_bytes=40 << 20),
        cost_estimate=pl.CostEstimate(flops=1_000_000, bytes_accessed=1_000_000, transcendentals=0),
    )(jnp.stack([base, choice]).astype(jnp.int32), *bases, *choices, *arrivals)


def assemble_kernel(place_ref, own_ref, sibling_ref, *refs):
    coded_refs, out_ref = refs[:-1], refs[-1]
    flip = pl.program_id(0) ^ place_ref[0]

    @pl.when(flip == 0)
    def _():
        out_ref[...] = own_ref[...]

    @pl.when(flip == 1)
    def _():
        out_ref[...] = sibling_ref[...]

    for index, coded_ref in enumerate(coded_refs):

        @pl.when(flip == 2 + index)
        def _():
            out_ref[...] = decoded(coded_ref, out_ref.shape[0])


def assemble(place, own, sibling, *others):
    rows, cols = own.shape
    return pl.pallas_call(
        assemble_kernel,
        grid_spec=pltpu.PrefetchScalarGridSpec(
            num_scalar_prefetch=1,
            grid=(4,),
            in_specs=[pl.BlockSpec((rows, cols), lambda j, _: (0, 0))] * 2
            + [pl.BlockSpec((rows + TAIL, cols), lambda j, _: (0, 0))] * 2,
            out_specs=pl.BlockSpec((rows, cols), lambda j, _: (0, j)),
        ),
        out_shape=jax.ShapeDtypeStruct((rows, 4 * cols), F32),
        compiler_params=pltpu.CompilerParams(vmem_limit_bytes=40 << 20),
        cost_estimate=pl.CostEstimate(flops=1_000_000, bytes_accessed=1_000_000, transcendentals=0),
    )(place.astype(jnp.int32).reshape(1), own, sibling, *others)


def hole_kernel(count, places_ref, *refs):
    rows_refs, occ_ref = refs[:count], refs[count]
    out_ref, columns_ref = refs[-2:]
    part = rows_refs[0].shape[0]
    for index, rows_ref in enumerate(rows_refs):
        start = pl.multiple_of(places_ref[index] * part, part)
        columns_ref[pl.ds(start, part), :] = rows_ref[...]
    out_ref[...] = jnp.dot(occ_ref[...], columns_ref[...], preferred_element_type=F32)


def hole_product(occ, row_blocks, places, half):
    part, depth = row_blocks[0].shape
    cols = depth // 2
    width = min(cols, 512)
    steps = cols // width
    return pl.pallas_call(
        functools.partial(hole_kernel, len(row_blocks)),
        grid_spec=pltpu.PrefetchScalarGridSpec(
            num_scalar_prefetch=1,
            grid=(steps,),
            in_specs=[pl.BlockSpec((part, width), lambda j, scalars: (0, scalars[len(row_blocks)] * steps + j))] * len(row_blocks)
            + [pl.BlockSpec(occ.shape, lambda j, scalars: (0, 0))],
            out_specs=pl.BlockSpec((occ.shape[0], width), lambda j, scalars: (0, j)),
            scratch_shapes=[pltpu.VMEM((occ.shape[1], width), occ.dtype)],
        ),
        out_shape=jax.ShapeDtypeStruct((occ.shape[0], cols), F32),
        compiler_params=pltpu.CompilerParams(vmem_limit_bytes=32 << 20),
        cost_estimate=pl.CostEstimate(flops=2_000_000_000, bytes_accessed=2_000_000, transcendentals=0),
    )(jnp.stack([*places, half]).astype(jnp.int32), *row_blocks, occ)


def masked_rows(amplitudes, occ_irrep, virt_irrep):
    keep = occ_irrep[:, None] == virt_irrep[None, :]
    return jnp.where(keep, amplitudes, jnp.zeros_like(amplitudes))


def whole_sums(amplitudes, virt_integrals, occ_integrals, occ_irrep, virt_irrep):
    masked = masked_rows(amplitudes, occ_irrep, virt_irrep)
    rows = lax.all_gather(masked, ("gz", "gy"), axis=0, tiled=True)
    partial = jnp.dot(rows, virt_integrals, preferred_element_type=F32)
    nx, nz = lax.axis_size("gx"), lax.axis_size("gz")
    by_owner = partial.reshape(nz, nx, -1, partial.shape[1]).swapaxes(0, 1)
    mine = lax.psum_scatter(by_owner, "gx", scatter_dimension=0, tiled=True)
    ladder_term = lax.all_to_all(mine[0], "gz", split_axis=0, concat_axis=2, tiled=True)[0]
    width = rows.shape[1] // lax.axis_size("gy")
    columns = lax.dynamic_slice_in_dim(rows, lax.axis_index("gy") * width, width, 1)
    hole_term = jnp.dot(occ_integrals, columns, preferred_element_type=F32)
    return ladder_term, hole_term


def line_of_four(amplitudes, virt_integrals, occ_integrals, occ_irrep, virt_irrep):
    z, y, g = (lax.axis_index(name) for name in ("gx", "gy", "gz"))
    mirrored = z >= 2
    first = (y == 1) != mirrored
    inner = (z == 1) | (z == 2)
    part = amplitudes.shape[0] // 2

    def over_gz(value, flip):
        return lax.ppermute(value, "gz", [(i, i ^ flip) for i in range(4)])

    def sibling(value):
        return over_gz(value, 1)

    def over_gy(value):
        return lax.ppermute(value, "gy", [(0, 1), (1, 0)])

    def inward(code):
        return lax.ppermute(code, "gx", [(0, 1), (3, 2)])

    def across(code):
        return lax.ppermute(code, "gx", [(1, 2), (2, 1)])

    def outward(code):
        return lax.ppermute(code, "gx", [(2, 3), (1, 0)])

    def own_part(start):
        rows = lax.dynamic_slice_in_dim(amplitudes, start, part, 0)
        labels = lax.dynamic_slice_in_dim(occ_irrep, start, part, 0)
        return masked_rows(rows, labels, virt_irrep)

    def pick(condition, one, other):
        return jnp.where(condition, one, other)

    def stage(work):
        skipped = jax.tree.map(lambda leaf: jnp.zeros(leaf.shape, leaf.dtype), jax.eval_shape(work))
        return lax.cond(z < 4, work, lambda: skipped)

    def times(*pairs, swapped=jnp.bool_(False)):
        return products(pairs, virt_integrals, swapped)

    second = ~first
    none = jnp.int32(0)

    def plus(choices, bases):
        which = second if len(bases) == 2 else none
        return sums("coded", 1, bases, which, choices, which, [])[0]

    odd = pick(mirrored, 0, part)
    high, low = own_part(odd), own_part(part - odd)

    def work0():
        x_high, y_high, s_high = over_gz(high, 2), over_gy(high), sibling(high)
        (near,) = times((high, s_high))
        return x_high, y_high, s_high, near

    x_high, y_high, s_high, (q_high_near, p0) = stage(work0)

    def work1():
        a0, yx_high, y_low = inward(p0), over_gz(y_high, 2), over_gy(low)
        sx_high, sy_high = sibling(x_high), sibling(y_high)
        urgent, rest = times((x_high, sx_high), (y_high, sy_high), swapped=second)
        return a0, yx_high, y_low, sx_high, sy_high, urgent, rest

    a0, yx_high, y_low, sx_high, sy_high, (q_urgent, p1), (q_rest, p_rest) = stage(work1)
    two = pick(first, low, y_low)

    def work2():
        a1, x_two, syx_high, s_two = inward(p1), over_gz(two, 2), sibling(yx_high), sibling(two)
        (y_high_far, p_y_high_far), two_near = times((yx_high, syx_high), (two, s_two))
        zero = pick(first, y_low, low)
        return a1, x_two, syx_high, s_two, zero, y_high_far, two_near, pick(first, p_rest, p_y_high_far), pick(first, p_y_high_far, p_rest)

    a1, x_two, syx_high, s_two, zero, q_y_high_far, (q_two_near, p5), p2, p4 = stage(work2)

    def work3():
        a2, x_zero, sx_two, s_zero = inward(p2), over_gz(zero, 2), sibling(x_two), sibling(zero)
        b0 = across(plus([a0, a1], [q_high_near, q_urgent]))
        two_far, zero_near = times((x_two, sx_two), (zero, s_zero))
        return b0, a2, x_zero, sx_two, s_zero, two_far, zero_near[0]

    b0, a2, x_zero, sx_two, s_zero, (q_two_far, p3), q_zero_near = stage(work3)

    def work4():
        a3 = inward(p3)
        b1 = across(plus([a1, a2], [q_urgent, q_y_high_far]))
        c0 = outward(plus([b0], [q_zero_near]))
        sx_zero = sibling(x_zero)
        ((zero_far, _),) = times((x_zero, sx_zero))
        return a3, b1, c0, sx_zero, zero_far

    a3, b1, c0, sx_zero, q_zero_far = stage(work4)

    def work5():
        a4, b2, c1 = inward(p4), across(plus([a3], [q_two_far])), outward(plus([b1], [q_zero_far]))
        base = pick(inner, pick(first, 0, 1), 2)
        far = sums("coded", 2, [q_y_high_far, q_rest, q_zero_far], base, [], none, [a4, b2, c1])
        return far

    far_one, far_two = stage(work5)

    def owner(index):
        return pick(mirrored, 3 - index, index)

    held = (
        (owner(pick(first, 3, 1)), (high, s_high, x_high, sx_high)),
        (owner(pick(first, 1, 3)), (y_high, sy_high, yx_high, syx_high)),
        (owner(2), (two, s_two, x_two, sx_two)),
        (owner(0), (zero, s_zero, x_zero, sx_zero)),
    )
    row_blocks = [block for _, group in held for block in group]
    places = [(g ^ flip) * 4 + place for place, _ in held for flip in range(4)]

    def work6():
        a5, block_two, block_three = inward(p5), over_gz(far_one, 2), over_gz(far_two, 3)
        base = pick(inner, pick(first, 0, 1), 2)
        (almost,) = sums("plain", 1, [q_rest, q_high_near, q_zero_near], base, [a2, a0], second, [c0])
        hole_term = hole_product(occ_integrals, row_blocks, places, y)
        return a5, block_two, block_three, almost, hole_term

    a5, block_two, block_three, almost, hole_term = stage(work6)

    b3 = across(plus([a5], [q_two_near]))
    near_one, near_two = sums("plain", 2, [almost], none, [], none, [b3])
    ladder_term = assemble(g, near_one, sibling(near_two), block_two, block_three)
    return ladder_term, hole_term


def solution(mesh):
    placed = (P(("gz", "gy"), "gx"), P("gx", ("gy", "gz")), P("gz", None), P(("gz", "gy")), P("gx"))
    sizes = tuple(mesh.shape[name] for name in ("gx", "gy", "gz"))
    return jax.shard_map(
        line_of_four if sizes == (4, 2, 4) else whole_sums,
        mesh=mesh,
        in_specs=placed,
        out_specs=(P(("gz", "gx"), "gy"), P("gz", ("gx", "gy"))),
        check_vma=False,
    )
```

```python
import functools

import jax
import jax.numpy as jnp
from jax import lax
from jax.experimental import pallas as pl
from jax.experimental.pallas import tpu as pltpu
from jax.sharding import PartitionSpec as P

F32 = jnp.float32
CODE = jnp.int16
TAIL = 16
FINE = 64.0
LOG_TOP = 29.9
SMALLEST = 1e-27


def coded(value):
    largest = jnp.maximum(jnp.max(jnp.abs(value)), SMALLEST)
    level = jnp.ceil(jnp.log2(jnp.full((TAIL, value.shape[1]), largest, F32)) * FINE)
    factor = jnp.exp2(LOG_TOP - level[:1] * (1.0 / FINE))
    size = jnp.abs(value) * factor
    size = (size * lax.rsqrt(jnp.maximum(size, 1e-6)) + 0.5).astype(jnp.int32)
    return jnp.where(value < 0.0, -size, size).astype(CODE), level.astype(jnp.int32).astype(CODE)


def decoded(ref, rows):
    code = ref[:rows, :].astype(jnp.int32).astype(F32)
    level = ref[rows:, :].astype(jnp.int32).astype(F32)[:1]
    return code * jnp.abs(code) * jnp.exp2(level * (1.0 / FINE) - LOG_TOP)


def write_coded(ref, value, start, width):
    rows = value.shape[0]
    code, level = coded(value)
    ref[:rows, start:start + width] = code
    ref[rows:, start:start + width] = level


def products_kernel(count, order_ref, *refs):
    rows_refs, integrals_ref = refs[:2 * count], refs[2 * count]
    out_refs, code_refs = refs[2 * count + 1:3 * count + 1], refs[3 * count + 1:]
    rows, cols = 2 * rows_refs[0].shape[0], integrals_ref.shape[1]
    width = min(cols, 512)
    step, last = pl.program_id(0), pl.num_programs(0) - 1

    @pl.when(step == 0)
    def _():
        for out_ref in out_refs:
            out_ref[...] = jnp.zeros_like(out_ref)

    blocks = [rows_ref[...] for rows_ref in rows_refs]
    if count == 2:
        swapped = order_ref[0] == 1
        blocks = [jnp.where(swapped, blocks[(i + 2) % 4], blocks[i]) for i in range(4)]
    gathered = jnp.concatenate(blocks, axis=0)
    for start in range(0, cols, width):
        value = jnp.dot(gathered, integrals_ref[:, start:start + width], preferred_element_type=F32)
        for index, out_ref in enumerate(out_refs):
            out_ref[:, start:start + width] += value[rows * index:rows * (index + 1)]

    @pl.when(step == last)
    def _():
        for out_ref, code_ref in zip(out_refs, code_refs):
            for start in range(0, cols, width):
                write_coded(code_ref, out_ref[:, start:start + width], start, width)


def products(pairs, integrals, swapped):
    part, depth = pairs[0][0].shape
    count, cols = len(pairs), integrals.shape[1]
    block = min(depth, 1024)
    rows = 2 * part
    results = pl.pallas_call(
        functools.partial(products_kernel, count),
        grid_spec=pltpu.PrefetchScalarGridSpec(
            num_scalar_prefetch=1,
            grid=(depth // block,),
            in_specs=[pl.BlockSpec((part, block), lambda k, _: (0, k))] * (2 * count)
            + [pl.BlockSpec((block, cols), lambda k, _: (k, 0))],
            out_specs=[pl.BlockSpec((rows, cols), lambda k, _: (0, 0))] * count
            + [pl.BlockSpec((rows + TAIL, cols), lambda k, _: (0, 0))] * count,
        ),
        out_shape=[jax.ShapeDtypeStruct((rows, cols), F32)] * count
        + [jax.ShapeDtypeStruct((rows + TAIL, cols), CODE)] * count,
        compiler_params=pltpu.CompilerParams(vmem_limit_bytes=40 << 20),
        cost_estimate=pl.CostEstimate(flops=2_000_000_000, bytes_accessed=2_000_000, transcendentals=0),
    )(swapped.astype(jnp.int32).reshape(1), *[block for pair in pairs for block in pair], integrals)
    return list(zip(results[:count], results[count:]))


def sums_kernel(kind, bases, choices, arrivals, flags_ref, *refs):
    base_refs, refs = refs[:bases], refs[bases:]
    choice_refs, refs = refs[:choices], refs[choices:]
    arrival_refs, out_refs, total_ref = refs[:arrivals], refs[arrivals:-1], refs[-1]
    rows, width = total_ref.shape
    for index, base_ref in enumerate(base_refs):

        @pl.when(flags_ref[0] == index)
        def _():
            total_ref[...] = base_ref[...]

    for index, choice_ref in enumerate(choice_refs):

        @pl.when(flags_ref[1] == index)
        def _():
            total_ref[...] += decoded(choice_ref, rows)

    total = total_ref[...]
    for arrival_ref in arrival_refs:
        total += decoded(arrival_ref, rows)
    each = rows // len(out_refs)
    for index, out_ref in enumerate(out_refs):
        own = total[each * index:each * (index + 1)]
        if kind == "plain":
            out_ref[...] = own
        else:
            write_coded(out_ref, own, 0, width)


def sums(kind, outs, bases, base, choices, choice, arrivals):
    rows, cols = bases[0].shape
    width = min(cols, 512)
    each = rows // outs + (0 if kind == "plain" else TAIL)
    return pl.pallas_call(
        functools.partial(sums_kernel, kind, len(bases), len(choices), len(arrivals)),
        grid_spec=pltpu.PrefetchScalarGridSpec(
            num_scalar_prefetch=1,
            grid=(cols // width,),
            in_specs=[pl.BlockSpec((rows, width), lambda j, _: (0, j))] * len(bases)
            + [pl.BlockSpec((rows + TAIL, width), lambda j, _: (0, j))] * (len(choices) + len(arrivals)),
            out_specs=[pl.BlockSpec((each, width), lambda j, _: (0, j))] * outs,
            scratch_shapes=[pltpu.VMEM((rows, width), F32)],
        ),
        out_shape=[jax.ShapeDtypeStruct((each, cols), F32 if kind == "plain" else CODE)] * outs,
        compiler_params=pltpu.CompilerParams(vmem_limit_bytes=40 << 20),
        cost_estimate=pl.CostEstimate(flops=1_000_000, bytes_accessed=1_000_000, transcendentals=0),
    )(jnp.stack([base, choice]).astype(jnp.int32), *bases, *choices, *arrivals)


def assemble_kernel(place_ref, own_ref, sibling_ref, *refs):
    coded_refs, out_ref = refs[:-1], refs[-1]
    flip = pl.program_id(0) ^ place_ref[0]

    @pl.when(flip == 0)
    def _():
        out_ref[...] = own_ref[...]

    @pl.when(flip == 1)
    def _():
        out_ref[...] = sibling_ref[...]

    for index, coded_ref in enumerate(coded_refs):

        @pl.when(flip == 2 + index)
        def _():
            out_ref[...] = decoded(coded_ref, out_ref.shape[0])


def assemble(place, own, sibling, *others):
    rows, cols = own.shape
    return pl.pallas_call(
        assemble_kernel,
        grid_spec=pltpu.PrefetchScalarGridSpec(
            num_scalar_prefetch=1,
            grid=(4,),
            in_specs=[pl.BlockSpec((rows, cols), lambda j, _: (0, 0))] * 2
            + [pl.BlockSpec((rows + TAIL, cols), lambda j, _: (0, 0))] * 2,
            out_specs=pl.BlockSpec((rows, cols), lambda j, _: (0, j)),
        ),
        out_shape=jax.ShapeDtypeStruct((rows, 4 * cols), F32),
        compiler_params=pltpu.CompilerParams(vmem_limit_bytes=40 << 20),
        cost_estimate=pl.CostEstimate(flops=1_000_000, bytes_accessed=1_000_000, transcendentals=0),
    )(place.astype(jnp.int32).reshape(1), own, sibling, *others)


def hole_kernel(count, places_ref, *refs):
    rows_refs, occ_ref = refs[:count], refs[count]
    out_ref, columns_ref = refs[-2:]
    part = rows_refs[0].shape[0]
    for index, rows_ref in enumerate(rows_refs):
        start = pl.multiple_of(places_ref[index] * part, part)
        columns_ref[pl.ds(start, part), :] = rows_ref[...]
    out_ref[...] = jnp.dot(occ_ref[...], columns_ref[...], preferred_element_type=F32)


def hole_product(occ, row_blocks, places, half):
    part, depth = row_blocks[0].shape
    cols = depth // 2
    width = min(cols, 512)
    steps = cols // width
    return pl.pallas_call(
        functools.partial(hole_kernel, len(row_blocks)),
        grid_spec=pltpu.PrefetchScalarGridSpec(
            num_scalar_prefetch=1,
            grid=(steps,),
            in_specs=[pl.BlockSpec((part, width), lambda j, scalars: (0, scalars[len(row_blocks)] * steps + j))] * len(row_blocks)
            + [pl.BlockSpec(occ.shape, lambda j, scalars: (0, 0))],
            out_specs=pl.BlockSpec((occ.shape[0], width), lambda j, scalars: (0, j)),
            scratch_shapes=[pltpu.VMEM((occ.shape[1], width), occ.dtype)],
        ),
        out_shape=jax.ShapeDtypeStruct((occ.shape[0], cols), F32),
        compiler_params=pltpu.CompilerParams(vmem_limit_bytes=32 << 20),
        cost_estimate=pl.CostEstimate(flops=2_000_000_000, bytes_accessed=2_000_000, transcendentals=0),
    )(jnp.stack([*places, half]).astype(jnp.int32), *row_blocks, occ)


def masked_rows(amplitudes, occ_irrep, virt_irrep):
    keep = occ_irrep[:, None] == virt_irrep[None, :]
    return jnp.where(keep, amplitudes, jnp.zeros_like(amplitudes))


def whole_sums(amplitudes, virt_integrals, occ_integrals, occ_irrep, virt_irrep):
    masked = masked_rows(amplitudes, occ_irrep, virt_irrep)
    rows = lax.all_gather(masked, ("gz", "gy"), axis=0, tiled=True)
    partial = jnp.dot(rows, virt_integrals, preferred_element_type=F32)
    nx, nz = lax.axis_size("gx"), lax.axis_size("gz")
    by_owner = partial.reshape(nz, nx, -1, partial.shape[1]).swapaxes(0, 1)
    mine = lax.psum_scatter(by_owner, "gx", scatter_dimension=0, tiled=True)
    ladder_term = lax.all_to_all(mine[0], "gz", split_axis=0, concat_axis=2, tiled=True)[0]
    width = rows.shape[1] // lax.axis_size("gy")
    columns = lax.dynamic_slice_in_dim(rows, lax.axis_index("gy") * width, width, 1)
    hole_term = jnp.dot(occ_integrals, columns, preferred_element_type=F32)
    return ladder_term, hole_term


def line_of_four(amplitudes, virt_integrals, occ_integrals, occ_irrep, virt_irrep):
    z, y, g = (lax.axis_index(name) for name in ("gx", "gy", "gz"))
    mirrored = z >= 2
    first = (y == 1) != mirrored
    inner = (z == 1) | (z == 2)
    part = amplitudes.shape[0] // 2

    def over_gz(value, flip):
        return lax.ppermute(value, "gz", [(i, i ^ flip) for i in range(4)])

    def sibling(value):
        return over_gz(value, 1)

    def over_gy(value):
        return lax.ppermute(value, "gy", [(0, 1), (1, 0)])

    def inward(code):
        return lax.ppermute(code, "gx", [(0, 1), (3, 2)])

    def across(code):
        return lax.ppermute(code, "gx", [(1, 2), (2, 1)])

    def inward_two(code):
        return lax.ppermute(code, "gx", [(0, 2), (3, 1)])

    def outward(code):
        return lax.ppermute(code, "gx", [(2, 3), (1, 0)])

    def own_part(start):
        rows = lax.dynamic_slice_in_dim(amplitudes, start, part, 0)
        labels = lax.dynamic_slice_in_dim(occ_irrep, start, part, 0)
        return masked_rows(rows, labels, virt_irrep)

    def pick(condition, one, other):
        return jnp.where(condition, one, other)

    def stage(work):
        skipped = jax.tree.map(lambda leaf: jnp.zeros(leaf.shape, leaf.dtype), jax.eval_shape(work))
        return lax.cond(z < 4, work, lambda: skipped)

    def times(*pairs, swapped=jnp.bool_(False)):
        return products(pairs, virt_integrals, swapped)

    second = ~first
    none = jnp.int32(0)

    def plus(choices, bases):
        which = second if len(bases) == 2 else none
        return sums("coded", 1, bases, which, choices, which, [])[0]

    odd = pick(mirrored, 0, part)
    high, low = own_part(odd), own_part(part - odd)

    def work0():
        x_high, y_high, s_high = over_gz(high, 2), over_gy(high), sibling(high)
        (near,) = times((high, s_high))
        return x_high, y_high, s_high, near

    x_high, y_high, s_high, (q_high_near, p0) = stage(work0)

    def work1():
        a0, yx_high, y_low = inward(p0), over_gz(y_high, 2), over_gy(low)
        sx_high, sy_high = sibling(x_high), sibling(y_high)
        urgent, rest = times((x_high, sx_high), (y_high, sy_high), swapped=second)
        return a0, yx_high, y_low, sx_high, sy_high, urgent, rest

    a0, yx_high, y_low, sx_high, sy_high, (q_urgent, p1), (q_rest, p_rest) = stage(work1)
    two = pick(first, low, y_low)

    def work2():
        a1, x_two, syx_high, s_two = inward(p1), over_gz(two, 2), sibling(yx_high), sibling(two)
        (y_high_far, p_y_high_far), two_near = times((yx_high, syx_high), (two, s_two))
        zero = pick(first, y_low, low)
        return a1, x_two, syx_high, s_two, zero, y_high_far, two_near, pick(first, p_rest, p_y_high_far), pick(first, p_y_high_far, p_rest)

    a1, x_two, syx_high, s_two, zero, q_y_high_far, (q_two_near, p5), p2, p4 = stage(work2)

    def work3():
        a2, m_near, x_zero, sx_two = inward(p2), across(p5), over_gz(zero, 2), sibling(x_two)
        b0 = plus([a0, a1], [q_high_near, q_urgent])
        (two_far,) = times((x_two, sx_two))
        return a2, m_near, x_zero, sx_two, b0, two_far

    a2, m_near, x_zero, sx_two, p_b0, (q_two_far, p3) = stage(work3)

    def work4():
        a3, b0, s_zero = inward(p3), across(p_b0), sibling(zero)
        b1 = plus([a1, a2], [q_urgent, q_y_high_far])
        ((zero_near, _),) = times((zero, s_zero))
        return a3, b0, s_zero, b1, zero_near

    a3, b0, s_zero, p_b1, q_zero_near = stage(work4)

    def work5():
        a4, b1, sx_zero = inward(p4), across(p_b1), sibling(x_zero)
        b2 = plus([a3], [q_two_far])
        ((zero_far, _),) = times((x_zero, sx_zero))
        return a4, b1, sx_zero, b2, zero_far

    a4, b1, sx_zero, p_b2, q_zero_far = stage(work5)

    def work6():
        b2 = across(p_b2)
        c1 = outward(plus([b1], [q_zero_far]))
        base = pick(inner, pick(first, 0, 1), 2)
        (far,) = sums("plain", 1, [q_y_high_far, q_rest, q_zero_far], base, [], none, [a4])
        c0 = plus([b0], [q_zero_near])
        return (c0, *sums("coded", 2, [far], none, [], none, [b2, c1]))

    p_c0, far_one, far_two = stage(work6)

    def owner(index):
        return pick(mirrored, 3 - index, index)

    held = (
        (owner(pick(first, 3, 1)), (high, s_high, x_high, sx_high)),
        (owner(pick(first, 1, 3)), (y_high, sy_high, yx_high, syx_high)),
        (owner(2), (two, s_two, x_two, sx_two)),
        (owner(0), (zero, s_zero, x_zero, sx_zero)),
    )
    row_blocks = [block for _, group in held for block in group]
    places = [(g ^ flip) * 4 + place for place, _ in held for flip in range(4)]

    def work7():
        e_near, c0, block_two, block_three = inward_two(p5), outward(p_c0), over_gz(far_one, 2), over_gz(far_two, 3)
        base = pick(inner, pick(first, 0, 1), 2)
        (almost,) = sums("plain", 1, [q_rest, q_high_near, q_zero_near], base, [a2, a0], second, [m_near])
        hole_term = hole_product(occ_integrals, row_blocks, places, y)
        return (block_two, block_three, hole_term, *sums("plain", 2, [almost], none, [], none, [e_near, c0]))

    block_two, block_three, hole_term, near_one, near_two = stage(work7)
    ladder_term = assemble(g, near_one, sibling(near_two), block_two, block_three)
    return ladder_term, hole_term


def solution(mesh):
    placed = (P(("gz", "gy"), "gx"), P("gx", ("gy", "gz")), P("gz", None), P(("gz", "gy")), P("gx"))
    sizes = tuple(mesh.shape[name] for name in ("gx", "gy", "gz"))
    return jax.shard_map(
        line_of_four if sizes == (4, 2, 4) else whole_sums,
        mesh=mesh,
        in_specs=placed,
        out_specs=(P(("gz", "gx"), "gy"), P("gz", ("gx", "gy"))),
        check_vma=False,
    )
```

```python
import functools

import jax
import jax.numpy as jnp
from jax import lax
from jax.experimental import pallas as pl
from jax.experimental.pallas import tpu as pltpu
from jax.sharding import PartitionSpec as P

F32 = jnp.float32
CODE = jnp.int16
TAIL = 16
FINE = 64.0
LOG_TOP = 29.9
SMALLEST = 1e-27


def coded(value):
    largest = jnp.maximum(jnp.max(jnp.abs(value)), SMALLEST)
    level = jnp.ceil(jnp.log2(jnp.full((TAIL, value.shape[1]), largest, F32)) * FINE)
    factor = jnp.exp2(LOG_TOP - level[:1] * (1.0 / FINE))
    size = jnp.abs(value) * factor
    size = (size * lax.rsqrt(jnp.maximum(size, 1e-6)) + 0.5).astype(jnp.int32)
    return jnp.where(value < 0.0, -size, size).astype(CODE), level.astype(jnp.int32).astype(CODE)


def decoded(ref, rows):
    code = ref[:rows, :].astype(jnp.int32).astype(F32)
    level = ref[rows:, :].astype(jnp.int32).astype(F32)[:1]
    return code * jnp.abs(code) * jnp.exp2(level * (1.0 / FINE) - LOG_TOP)


def write_coded(ref, value, start, width):
    rows = value.shape[0]
    code, level = coded(value)
    ref[:rows, start:start + width] = code
    ref[rows:, start:start + width] = level


def products_kernel(options, flag_ref, *refs):
    count, inputs = len(options), 2 * sum(options)
    rows_refs, integrals_ref = refs[:inputs], refs[inputs]
    out_refs, code_refs = refs[inputs + 1:inputs + count + 1], refs[inputs + count + 1:]
    rows, cols = 2 * rows_refs[0].shape[0], integrals_ref.shape[1]
    width = min(cols, 512)
    step, last = pl.program_id(0), pl.num_programs(0) - 1

    @pl.when(step == 0)
    def _():
        for out_ref in out_refs:
            out_ref[...] = jnp.zeros_like(out_ref)

    blocks, at = [], 0
    for option in options:
        pair = [rows_ref[...] for rows_ref in rows_refs[at:at + 2]]
        if option == 2:
            pair = [jnp.where(flag_ref[0] == 1, one, rows_refs[at + 2 + i][...]) for i, one in enumerate(pair)]
        blocks += pair
        at += 2 * option
    gathered = jnp.concatenate(blocks, axis=0)
    for start in range(0, cols, width):
        value = jnp.dot(gathered, integrals_ref[:, start:start + width], preferred_element_type=F32)
        for index, out_ref in enumerate(out_refs):
            out_ref[:, start:start + width] += value[rows * index:rows * (index + 1)]

    @pl.when(step == last)
    def _():
        for out_ref, code_ref in zip(out_refs, code_refs):
            for start in range(0, cols, width):
                write_coded(code_ref, out_ref[:, start:start + width], start, width)


def products(groups, integrals, flag):
    part, depth = groups[0][0][0].shape
    options, cols = [len(group) for group in groups], integrals.shape[1]
    blocks = [block for group in groups for pair in group for block in pair]
    block, count, rows = min(depth, 1024), len(groups), 2 * part
    results = pl.pallas_call(
        functools.partial(products_kernel, options),
        grid_spec=pltpu.PrefetchScalarGridSpec(
            num_scalar_prefetch=1,
            grid=(depth // block,),
            in_specs=[pl.BlockSpec((part, block), lambda k, _: (0, k))] * len(blocks)
            + [pl.BlockSpec((block, cols), lambda k, _: (k, 0))],
            out_specs=[pl.BlockSpec((rows, cols), lambda k, _: (0, 0))] * count
            + [pl.BlockSpec((rows + TAIL, cols), lambda k, _: (0, 0))] * count,
        ),
        out_shape=[jax.ShapeDtypeStruct((rows, cols), F32)] * count
        + [jax.ShapeDtypeStruct((rows + TAIL, cols), CODE)] * count,
        compiler_params=pltpu.CompilerParams(vmem_limit_bytes=40 << 20),
        cost_estimate=pl.CostEstimate(flops=2_000_000_000, bytes_accessed=2_000_000, transcendentals=0),
    )(flag.astype(jnp.int32).reshape(1), *blocks, integrals)
    return list(zip(results[:count], results[count:]))


def sums_kernel(kind, bases, choices, arrivals, flags_ref, *refs):
    base_refs, refs = refs[:bases], refs[bases:]
    choice_refs, refs = refs[:choices], refs[choices:]
    arrival_refs, out_refs, total_ref = refs[:arrivals], refs[arrivals:-1], refs[-1]
    rows, width = total_ref.shape
    for index, base_ref in enumerate(base_refs):

        @pl.when(flags_ref[0] == index)
        def _():
            total_ref[...] = base_ref[...]

    for index, choice_ref in enumerate(choice_refs):

        @pl.when(flags_ref[1] == index)
        def _():
            total_ref[...] += decoded(choice_ref, rows)

    total = total_ref[...]
    for arrival_ref in arrival_refs:
        total += decoded(arrival_ref, rows)
    each = rows // len(out_refs)
    for index, out_ref in enumerate(out_refs):
        own = total[each * index:each * (index + 1)]
        if kind == "plain":
            out_ref[...] = own
        else:
            write_coded(out_ref, own, 0, width)


def sums(kind, outs, bases, base, choices, choice, arrivals):
    rows, cols = bases[0].shape
    width = min(cols, 512)
    each = rows // outs + (0 if kind == "plain" else TAIL)
    return pl.pallas_call(
        functools.partial(sums_kernel, kind, len(bases), len(choices), len(arrivals)),
        grid_spec=pltpu.PrefetchScalarGridSpec(
            num_scalar_prefetch=1,
            grid=(cols // width,),
            in_specs=[pl.BlockSpec((rows, width), lambda j, _: (0, j))] * len(bases)
            + [pl.BlockSpec((rows + TAIL, width), lambda j, _: (0, j))] * (len(choices) + len(arrivals)),
            out_specs=[pl.BlockSpec((each, width), lambda j, _: (0, j))] * outs,
            scratch_shapes=[pltpu.VMEM((rows, width), F32)],
        ),
        out_shape=[jax.ShapeDtypeStruct((each, cols), F32 if kind == "plain" else CODE)] * outs,
        compiler_params=pltpu.CompilerParams(vmem_limit_bytes=40 << 20),
        cost_estimate=pl.CostEstimate(flops=1_000_000, bytes_accessed=1_000_000, transcendentals=0),
    )(jnp.stack([base, choice]).astype(jnp.int32), *bases, *choices, *arrivals)


def assemble_kernel(place_ref, own_ref, sibling_ref, *refs):
    coded_refs, out_ref = refs[:-1], refs[-1]
    flip = pl.program_id(0) ^ place_ref[0]

    @pl.when(flip == 0)
    def _():
        out_ref[...] = own_ref[...]

    @pl.when(flip == 1)
    def _():
        out_ref[...] = sibling_ref[...]

    for index, coded_ref in enumerate(coded_refs):

        @pl.when(flip == 2 + index)
        def _():
            out_ref[...] = decoded(coded_ref, out_ref.shape[0])


def assemble(place, own, sibling, *others):
    rows, cols = own.shape
    return pl.pallas_call(
        assemble_kernel,
        grid_spec=pltpu.PrefetchScalarGridSpec(
            num_scalar_prefetch=1,
            grid=(4,),
            in_specs=[pl.BlockSpec((rows, cols), lambda j, _: (0, 0))] * 2
            + [pl.BlockSpec((rows + TAIL, cols), lambda j, _: (0, 0))] * 2,
            out_specs=pl.BlockSpec((rows, cols), lambda j, _: (0, j)),
        ),
        out_shape=jax.ShapeDtypeStruct((rows, 4 * cols), F32),
        compiler_params=pltpu.CompilerParams(vmem_limit_bytes=40 << 20),
        cost_estimate=pl.CostEstimate(flops=1_000_000, bytes_accessed=1_000_000, transcendentals=0),
    )(place.astype(jnp.int32).reshape(1), own, sibling, *others)


def hole_kernel(count, places_ref, *refs):
    rows_refs, occ_ref = refs[:count], refs[count]
    out_ref, columns_ref = refs[-2:]
    part = rows_refs[0].shape[0]
    for index, rows_ref in enumerate(rows_refs):
        start = pl.multiple_of(places_ref[index] * part, part)
        columns_ref[pl.ds(start, part), :] = rows_ref[...]
    out_ref[...] = jnp.dot(occ_ref[...], columns_ref[...], preferred_element_type=F32)


def hole_product(occ, row_blocks, places, half):
    part, depth = row_blocks[0].shape
    cols = depth // 2
    width = min(cols, 512)
    steps = cols // width
    return pl.pallas_call(
        functools.partial(hole_kernel, len(row_blocks)),
        grid_spec=pltpu.PrefetchScalarGridSpec(
            num_scalar_prefetch=1,
            grid=(steps,),
            in_specs=[pl.BlockSpec((part, width), lambda j, scalars: (0, scalars[len(row_blocks)] * steps + j))] * len(row_blocks)
            + [pl.BlockSpec(occ.shape, lambda j, scalars: (0, 0))],
            out_specs=pl.BlockSpec((occ.shape[0], width), lambda j, scalars: (0, j)),
            scratch_shapes=[pltpu.VMEM((occ.shape[1], width), occ.dtype)],
        ),
        out_shape=jax.ShapeDtypeStruct((occ.shape[0], cols), F32),
        compiler_params=pltpu.CompilerParams(vmem_limit_bytes=32 << 20),
        cost_estimate=pl.CostEstimate(flops=2_000_000_000, bytes_accessed=2_000_000, transcendentals=0),
    )(jnp.stack([*places, half]).astype(jnp.int32), *row_blocks, occ)


def masked_rows(amplitudes, occ_irrep, virt_irrep):
    keep = occ_irrep[:, None] == virt_irrep[None, :]
    return jnp.where(keep, amplitudes, jnp.zeros_like(amplitudes))


def whole_sums(amplitudes, virt_integrals, occ_integrals, occ_irrep, virt_irrep):
    masked = masked_rows(amplitudes, occ_irrep, virt_irrep)
    rows = lax.all_gather(masked, ("gz", "gy"), axis=0, tiled=True)
    partial = jnp.dot(rows, virt_integrals, preferred_element_type=F32)
    nx, nz = lax.axis_size("gx"), lax.axis_size("gz")
    by_owner = partial.reshape(nz, nx, -1, partial.shape[1]).swapaxes(0, 1)
    mine = lax.psum_scatter(by_owner, "gx", scatter_dimension=0, tiled=True)
    ladder_term = lax.all_to_all(mine[0], "gz", split_axis=0, concat_axis=2, tiled=True)[0]
    width = rows.shape[1] // lax.axis_size("gy")
    columns = lax.dynamic_slice_in_dim(rows, lax.axis_index("gy") * width, width, 1)
    hole_term = jnp.dot(occ_integrals, columns, preferred_element_type=F32)
    return ladder_term, hole_term


def line_of_four(amplitudes, virt_integrals, occ_integrals, occ_irrep, virt_irrep):
    z, y, g = (lax.axis_index(name) for name in ("gx", "gy", "gz"))
    mirrored = z >= 2
    first = (y == 1) != mirrored
    inner = (z == 1) | (z == 2)
    part = amplitudes.shape[0] // 2

    def over_gz(value, flip):
        return lax.ppermute(value, "gz", [(i, i ^ flip) for i in range(4)])

    def sibling(value):
        return over_gz(value, 1)

    def over_gy(value):
        return lax.ppermute(value, "gy", [(0, 1), (1, 0)])

    def inward(code):
        return lax.ppermute(code, "gx", [(0, 1), (3, 2)])

    def across(code):
        return lax.ppermute(code, "gx", [(1, 2), (2, 1)])

    def inward_two(code):
        return lax.ppermute(code, "gx", [(0, 2), (3, 1)])

    def outward_two(code):
        return lax.ppermute(code, "gx", [(1, 3), (2, 0)])

    def outward(code):
        return lax.ppermute(code, "gx", [(2, 3), (1, 0)])

    def own_part(start):
        rows = lax.dynamic_slice_in_dim(amplitudes, start, part, 0)
        labels = lax.dynamic_slice_in_dim(occ_irrep, start, part, 0)
        return masked_rows(rows, labels, virt_irrep)

    def pick(condition, one, other):
        return jnp.where(condition, one, other)

    def stage(work):
        skipped = jax.tree.map(lambda leaf: jnp.zeros(leaf.shape, leaf.dtype), jax.eval_shape(work))
        return lax.cond(z < 4, work, lambda: skipped)

    def times(*groups):
        return products(groups, virt_integrals, first)

    second = ~first
    none = jnp.int32(0)

    def plus(choices, bases):
        which = second if len(bases) == 2 else none
        return sums("coded", 1, bases, which, choices, which, [])[0]

    odd = pick(mirrored, 0, part)
    high, low = own_part(odd), own_part(part - odd)

    def work0():
        x_high, y_high, s_high = over_gz(high, 2), over_gy(high), sibling(high)
        (near,) = times([(high, s_high)])
        return x_high, y_high, s_high, near

    x_high, y_high, s_high, (q_near, p0) = stage(work0)

    def work1():
        a0, yx_high, y_low = inward(p0), over_gz(y_high, 2), over_gy(low)
        sx_high, sy_high = sibling(x_high), sibling(y_high)
        (after,) = times([(x_high, sx_high), (y_high, sy_high)])
        return a0, yx_high, y_low, sx_high, sy_high, after

    a0, yx_high, y_low, sx_high, sy_high, (q_after, p1) = stage(work1)
    two = pick(first, low, y_low)

    def work2():
        a1, x_two, syx_high, s_two = inward(p1), over_gz(two, 2), sibling(yx_high), sibling(two)
        third, two_near = times([(y_high, sy_high), (yx_high, syx_high)], [(two, s_two)])
        return a1, x_two, syx_high, s_two, pick(first, y_low, low), third, two_near[1]

    a1, x_two, syx_high, s_two, zero, (q_third, p2), p5 = stage(work2)

    def work3():
        a2, m_near, x_zero, sx_two = inward(p2), across(p5), over_gz(zero, 2), sibling(x_two)
        b0 = plus([a0, a1], [q_near, q_after])
        (two_far,) = times([(x_two, sx_two)])
        return a2, m_near, x_zero, sx_two, b0, two_far

    a2, m_near, x_zero, sx_two, p_b0, (q_two_far, p3) = stage(work3)

    def work4():
        a3, b0, s_zero, sx_zero = inward(p3), outward_two(p_b0), sibling(zero), sibling(x_zero)
        b1 = plus([a1, a2], [q_after, q_third])
        (rest,) = times([(yx_high, syx_high), (x_high, sx_high)])
        return a3, b0, s_zero, sx_zero, b1, rest

    a3, b0, s_zero, sx_zero, p_b1, (q_rest, p4) = stage(work4)

    def work5():
        a4, b1 = inward(p4), outward_two(p_b1)
        b2 = plus([a3], [q_two_far])
        (zero_far,) = times([(x_zero, sx_zero)])
        return a4, b1, b2, zero_far

    a4, b1, p_b2, (q_zero_far, p6) = stage(work5)
    ends = pick(inner, 0, 1)

    def work6():
        b2, o_far = across(p_b2), outward(p6)
        (zero_near,) = times([(zero, s_zero)])
        (far,) = sums("plain", 1, [q_rest, q_zero_far], ends, [a4, b1], ends, [])
        return zero_near, sums("coded", 2, [far], none, [b2, o_far], ends, [])

    (q_zero_near, p7), (far_one, far_two) = stage(work6)

    def owner(index):
        return pick(mirrored, 3 - index, index)

    held = (
        (owner(pick(first, 3, 1)), (high, s_high, x_high, sx_high)),
        (owner(pick(first, 1, 3)), (y_high, sy_high, yx_high, syx_high)),
        (owner(2), (two, s_two, x_two, sx_two)),
        (owner(0), (zero, s_zero, x_zero, sx_zero)),
    )
    row_blocks = [block for _, group in held for block in group]
    places = [(g ^ flip) * 4 + place for place, _ in held for flip in range(4)]

    def work7():
        e_near, o_near, block_two, block_three = inward_two(p5), outward(p7), over_gz(far_one, 2), over_gz(far_two, 3)
        base = pick(inner, pick(first, 0, 1), 2)
        (almost,) = sums("plain", 1, [q_third, q_near, q_zero_near], base, [a2, a0, b0], base, [m_near])
        hole_term = hole_product(occ_integrals, row_blocks, places, y)
        return (block_two, block_three, hole_term, *sums("plain", 2, [almost], none, [e_near, o_near], ends, []))

    block_two, block_three, hole_term, near_one, near_two = stage(work7)
    ladder_term = assemble(g, near_one, sibling(near_two), block_two, block_three)
    return ladder_term, hole_term


def solution(mesh):
    placed = (P(("gz", "gy"), "gx"), P("gx", ("gy", "gz")), P("gz", None), P(("gz", "gy")), P("gx"))
    sizes = tuple(mesh.shape[name] for name in ("gx", "gy", "gz"))
    return jax.shard_map(
        line_of_four if sizes == (4, 2, 4) else whole_sums,
        mesh=mesh,
        in_specs=placed,
        out_specs=(P(("gz", "gx"), "gy"), P("gz", ("gx", "gy"))),
        check_vma=False,
    )
```

```python
import functools

import jax
import jax.numpy as jnp
from jax import lax
from jax.experimental import pallas as pl
from jax.experimental.pallas import tpu as pltpu
from jax.sharding import PartitionSpec as P

F32 = jnp.float32
CODE = jnp.int16
TAIL = 16
FINE = 64.0
LOG_TOP = 29.9
SMALLEST = 1e-27


def coded(value):
    largest = jnp.maximum(jnp.max(jnp.abs(value)), SMALLEST)
    level = jnp.ceil(jnp.log2(jnp.full((TAIL, value.shape[1]), largest, F32)) * FINE)
    factor = jnp.exp2(LOG_TOP - level[:1] * (1.0 / FINE))
    size = jnp.abs(value) * factor
    size = (size * lax.rsqrt(jnp.maximum(size, 1e-6)) + 0.5).astype(jnp.int32)
    return jnp.where(value < 0.0, -size, size).astype(CODE), level.astype(jnp.int32).astype(CODE)


def decoded(ref, rows):
    code = ref[:rows, :].astype(jnp.int32).astype(F32)
    level = ref[rows:, :].astype(jnp.int32).astype(F32)[:1]
    return code * jnp.abs(code) * jnp.exp2(level * (1.0 / FINE) - LOG_TOP)


def write_coded(ref, value, start, width):
    rows = value.shape[0]
    code, level = coded(value)
    ref[:rows, start:start + width] = code
    ref[rows:, start:start + width] = level


def products_kernel(options, flag_ref, *refs):
    count, inputs = len(options), 2 * sum(options)
    rows_refs, integrals_ref = refs[:inputs], refs[inputs]
    out_refs, code_refs = refs[inputs + 1:inputs + count + 1], refs[inputs + count + 1:]
    rows, cols = 2 * rows_refs[0].shape[0], integrals_ref.shape[1]
    width = min(cols, 512)
    step, last = pl.program_id(0), pl.num_programs(0) - 1

    @pl.when(step == 0)
    def _():
        for out_ref in out_refs:
            out_ref[...] = jnp.zeros_like(out_ref)

    blocks, at = [], 0
    for option in options:
        pair = [rows_ref[...] for rows_ref in rows_refs[at:at + 2]]
        if option == 2:
            pair = [jnp.where(flag_ref[0] == 1, one, rows_refs[at + 2 + i][...]) for i, one in enumerate(pair)]
        blocks += pair
        at += 2 * option
    gathered = jnp.concatenate(blocks, axis=0)
    for start in range(0, cols, width):
        value = jnp.dot(gathered, integrals_ref[:, start:start + width], preferred_element_type=F32)
        for index, out_ref in enumerate(out_refs):
            out_ref[:, start:start + width] += value[rows * index:rows * (index + 1)]

    @pl.when(step == last)
    def _():
        for out_ref, code_ref in zip(out_refs, code_refs):
            for start in range(0, cols, width):
                write_coded(code_ref, out_ref[:, start:start + width], start, width)


def products(groups, integrals, flag):
    part, depth = groups[0][0][0].shape
    options, cols = [len(group) for group in groups], integrals.shape[1]
    blocks = [block for group in groups for pair in group for block in pair]
    block, count, rows = min(depth, 1024), len(groups), 2 * part
    results = pl.pallas_call(
        functools.partial(products_kernel, options),
        grid_spec=pltpu.PrefetchScalarGridSpec(
            num_scalar_prefetch=1,
            grid=(depth // block,),
            in_specs=[pl.BlockSpec((part, block), lambda k, _: (0, k))] * len(blocks)
            + [pl.BlockSpec((block, cols), lambda k, _: (k, 0))],
            out_specs=[pl.BlockSpec((rows, cols), lambda k, _: (0, 0))] * count
            + [pl.BlockSpec((rows + TAIL, cols), lambda k, _: (0, 0))] * count,
        ),
        out_shape=[jax.ShapeDtypeStruct((rows, cols), F32)] * count
        + [jax.ShapeDtypeStruct((rows + TAIL, cols), CODE)] * count,
        compiler_params=pltpu.CompilerParams(vmem_limit_bytes=52 << 20),
        cost_estimate=pl.CostEstimate(flops=1_000_000, bytes_accessed=1_000_000, transcendentals=0),
    )(flag.astype(jnp.int32).reshape(1), *blocks, integrals)
    return list(zip(results[:count], results[count:]))


def sums_kernel(kind, bases, choices, arrivals, flags_ref, *refs):
    base_refs, refs = refs[:bases], refs[bases:]
    choice_refs, refs = refs[:choices], refs[choices:]
    arrival_refs, out_refs, total_ref = refs[:arrivals], refs[arrivals:-1], refs[-1]
    rows, width = total_ref.shape
    for index, base_ref in enumerate(base_refs):

        @pl.when(flags_ref[0] == index)
        def _():
            total_ref[...] = base_ref[...]

    for index, choice_ref in enumerate(choice_refs):

        @pl.when(flags_ref[1] == index)
        def _():
            total_ref[...] += decoded(choice_ref, rows)

    total = total_ref[...]
    for arrival_ref in arrival_refs:
        total += decoded(arrival_ref, rows)
    each = rows // len(out_refs)
    for index, out_ref in enumerate(out_refs):
        own = total[each * index:each * (index + 1)]
        if kind == "plain":
            out_ref[...] = own
        else:
            write_coded(out_ref, own, 0, width)


def sums(kind, outs, bases, base, choices, choice, arrivals):
    rows, cols = bases[0].shape
    width = min(cols, 512)
    each = rows // outs + (0 if kind == "plain" else TAIL)
    return pl.pallas_call(
        functools.partial(sums_kernel, kind, len(bases), len(choices), len(arrivals)),
        grid_spec=pltpu.PrefetchScalarGridSpec(
            num_scalar_prefetch=1,
            grid=(cols // width,),
            in_specs=[pl.BlockSpec((rows, width), lambda j, _: (0, j))] * len(bases)
            + [pl.BlockSpec((rows + TAIL, width), lambda j, _: (0, j))] * (len(choices) + len(arrivals)),
            out_specs=[pl.BlockSpec((each, width), lambda j, _: (0, j))] * outs,
            scratch_shapes=[pltpu.VMEM((rows, width), F32)],
        ),
        out_shape=[jax.ShapeDtypeStruct((each, cols), F32 if kind == "plain" else CODE)] * outs,
        compiler_params=pltpu.CompilerParams(vmem_limit_bytes=52 << 20),
        cost_estimate=pl.CostEstimate(flops=1_000_000, bytes_accessed=1_000_000, transcendentals=0),
    )(jnp.stack([base, choice]).astype(jnp.int32), *bases, *choices, *arrivals)


def assemble_kernel(place_ref, own_ref, sibling_ref, *refs):
    coded_refs, out_ref = refs[:-1], refs[-1]
    flip = pl.program_id(0) ^ place_ref[0]

    @pl.when(flip == 0)
    def _():
        out_ref[...] = own_ref[...]

    @pl.when(flip == 1)
    def _():
        out_ref[...] = sibling_ref[...]

    for index, coded_ref in enumerate(coded_refs):

        @pl.when(flip == 2 + index)
        def _():
            out_ref[...] = decoded(coded_ref, out_ref.shape[0])


def assemble(place, own, sibling, *others):
    rows, cols = own.shape
    return pl.pallas_call(
        assemble_kernel,
        grid_spec=pltpu.PrefetchScalarGridSpec(
            num_scalar_prefetch=1,
            grid=(4,),
            in_specs=[pl.BlockSpec((rows, cols), lambda j, _: (0, 0))] * 2
            + [pl.BlockSpec((rows + TAIL, cols), lambda j, _: (0, 0))] * 2,
            out_specs=pl.BlockSpec((rows, cols), lambda j, _: (0, j)),
        ),
        out_shape=jax.ShapeDtypeStruct((rows, 4 * cols), F32),
        compiler_params=pltpu.CompilerParams(vmem_limit_bytes=52 << 20),
        cost_estimate=pl.CostEstimate(flops=1_000_000, bytes_accessed=1_000_000, transcendentals=0),
    )(place.astype(jnp.int32).reshape(1), own, sibling, *others)


def hole_kernel(count, places_ref, *refs):
    rows_refs, occ_ref = refs[:count], refs[count]
    out_ref, columns_ref = refs[-2:]
    part = rows_refs[0].shape[0]
    for index, rows_ref in enumerate(rows_refs):
        start = pl.multiple_of(places_ref[index] * part, part)
        columns_ref[pl.ds(start, part), :] = rows_ref[...]
    out_ref[...] = jnp.dot(occ_ref[...], columns_ref[...], preferred_element_type=F32)


def hole_product(occ, row_blocks, places, half):
    part, depth = row_blocks[0].shape
    cols = depth // 2
    width = min(cols, 512)
    steps = cols // width
    return pl.pallas_call(
        functools.partial(hole_kernel, len(row_blocks)),
        grid_spec=pltpu.PrefetchScalarGridSpec(
            num_scalar_prefetch=1,
            grid=(steps,),
            in_specs=[pl.BlockSpec((part, width), lambda j, scalars: (0, scalars[len(row_blocks)] * steps + j))] * len(row_blocks)
            + [pl.BlockSpec(occ.shape, lambda j, scalars: (0, 0))],
            out_specs=pl.BlockSpec((occ.shape[0], width), lambda j, scalars: (0, j)),
            scratch_shapes=[pltpu.VMEM((occ.shape[1], width), occ.dtype)],
        ),
        out_shape=jax.ShapeDtypeStruct((occ.shape[0], cols), F32),
        compiler_params=pltpu.CompilerParams(vmem_limit_bytes=52 << 20),
        cost_estimate=pl.CostEstimate(flops=1_000_000, bytes_accessed=1_000_000, transcendentals=0),
    )(jnp.stack([*places, half]).astype(jnp.int32), *row_blocks, occ)


def masked_rows(amplitudes, occ_irrep, virt_irrep):
    keep = occ_irrep[:, None] == virt_irrep[None, :]
    return jnp.where(keep, amplitudes, jnp.zeros_like(amplitudes))


def whole_sums(amplitudes, virt_integrals, occ_integrals, occ_irrep, virt_irrep):
    masked = masked_rows(amplitudes, occ_irrep, virt_irrep)
    rows = lax.all_gather(masked, ("gz", "gy"), axis=0, tiled=True)
    partial = jnp.dot(rows, virt_integrals, preferred_element_type=F32)
    nx, nz = lax.axis_size("gx"), lax.axis_size("gz")
    by_owner = partial.reshape(nz, nx, -1, partial.shape[1]).swapaxes(0, 1)
    mine = lax.psum_scatter(by_owner, "gx", scatter_dimension=0, tiled=True)
    ladder_term = lax.all_to_all(mine[0], "gz", split_axis=0, concat_axis=2, tiled=True)[0]
    width = rows.shape[1] // lax.axis_size("gy")
    columns = lax.dynamic_slice_in_dim(rows, lax.axis_index("gy") * width, width, 1)
    hole_term = jnp.dot(occ_integrals, columns, preferred_element_type=F32)
    return ladder_term, hole_term


def line_of_four(amplitudes, virt_integrals, occ_integrals, occ_irrep, virt_irrep):
    z, y, g = (lax.axis_index(name) for name in ("gx", "gy", "gz"))
    mirrored = z >= 2
    first = (y == 1) != mirrored
    inner = (z == 1) | (z == 2)
    part = amplitudes.shape[0] // 2

    def over_gz(value, flip):
        return lax.ppermute(value, "gz", [(i, i ^ flip) for i in range(4)])

    def sibling(value):
        return over_gz(value, 1)

    def over_gy(value):
        return lax.ppermute(value, "gy", [(0, 1), (1, 0)])

    def inward(code):
        return lax.ppermute(code, "gx", [(0, 1), (3, 2)])

    def across(code):
        return lax.ppermute(code, "gx", [(1, 2), (2, 1)])

    def inward_two(code):
        return lax.ppermute(code, "gx", [(0, 2), (3, 1)])

    def outward_two(code):
        return lax.ppermute(code, "gx", [(1, 3), (2, 0)])

    def outward(code):
        return lax.ppermute(code, "gx", [(2, 3), (1, 0)])

    def own_part(start):
        rows = lax.dynamic_slice_in_dim(amplitudes, start, part, 0)
        labels = lax.dynamic_slice_in_dim(occ_irrep, start, part, 0)
        return masked_rows(rows, labels, virt_irrep)

    def pick(condition, one, other):
        return jnp.where(condition, one, other)

    def stage(work):
        skipped = jax.tree.map(lambda leaf: jnp.zeros(leaf.shape, leaf.dtype), jax.eval_shape(work))
        return lax.cond(z < 4, work, lambda: skipped)

    def times(*groups):
        return products(groups, virt_integrals, first)

    second = ~first
    none = jnp.int32(0)

    def plus(choices, bases):
        which = second if len(bases) == 2 else none
        return sums("coded", 1, bases, which, choices, which, [])[0]

    odd = pick(mirrored, 0, part)
    high, low = own_part(odd), own_part(part - odd)

    def work0():
        x_high, y_high, s_high = over_gz(high, 2), over_gy(high), sibling(high)
        (near,) = times([(high, s_high)])
        return x_high, y_high, s_high, near

    x_high, y_high, s_high, (q_near, p0) = stage(work0)

    def work1():
        a0, yx_high, y_low = inward(p0), over_gz(y_high, 2), over_gy(low)
        sx_high, sy_high = sibling(x_high), sibling(y_high)
        ((q_after, p1),) = times([(x_high, sx_high), (y_high, sy_high)])
        a1, syx_high = inward(p1), sibling(yx_high)
        two, zero = pick(first, low, y_low), pick(first, y_low, low)
        x_two, s_two = over_gz(two, 2), sibling(two)
        third, (_, p5) = times([(y_high, sy_high), (yx_high, syx_high)], [(two, s_two)])
        return a0, a1, yx_high, sx_high, sy_high, syx_high, two, zero, x_two, s_two, q_after, third, p5

    a0, a1, yx_high, sx_high, sy_high, syx_high, two, zero, x_two, s_two, q_after, (q_third, p2), p5 = stage(work1)

    def work2():
        a2, m_near, x_zero, sx_two, s_zero = inward(p2), across(p5), over_gz(zero, 2), sibling(x_two), sibling(zero)
        ((q_two_far, p3),) = times([(x_two, sx_two)])
        a3, b0 = inward(p3), outward_two(plus([a0, a1], [q_near, q_after]))
        (rest,) = times([(yx_high, syx_high), (x_high, sx_high)])
        b1 = plus([a1, a2], [q_after, q_third])
        return a2, m_near, x_zero, sx_two, s_zero, a3, b0, rest, b1, q_two_far

    a2, m_near, x_zero, sx_two, s_zero, a3, b0, (q_rest, p4), p_b1, q_two_far = stage(work2)
    ends = pick(inner, 0, 1)

    def work3():
        a4, b1, sx_zero = inward(p4), outward_two(p_b1), sibling(x_zero)
        b2 = across(plus([a3], [q_two_far]))
        ((q_zero_far, p6),) = times([(x_zero, sx_zero)])
        o_far = outward(p6)
        (zero_near,) = times([(zero, s_zero)])
        (far,) = sums("plain", 1, [q_rest, q_zero_far], ends, [a4, b1], ends, [])
        return sx_zero, zero_near, sums("coded", 2, [far], none, [b2, o_far], ends, [])

    sx_zero, (q_zero_near, p7), (far_one, far_two) = stage(work3)

    def owner(index):
        return pick(mirrored, 3 - index, index)

    held = (
        (owner(pick(first, 3, 1)), (high, s_high, x_high, sx_high)),
        (owner(pick(first, 1, 3)), (y_high, sy_high, yx_high, syx_high)),
        (owner(2), (two, s_two, x_two, sx_two)),
        (owner(0), (zero, s_zero, x_zero, sx_zero)),
    )
    row_blocks = [block for _, group in held for block in group]
    places = [(g ^ flip) * 4 + place for place, _ in held for flip in range(4)]

    def work4():
        e_near, o_near, block_two, block_three = inward_two(p5), outward(p7), over_gz(far_one, 2), over_gz(far_two, 3)
        base = pick(inner, pick(first, 0, 1), 2)
        (almost,) = sums("plain", 1, [q_third, q_near, q_zero_near], base, [a2, a0, b0], base, [m_near])
        hole_term = hole_product(occ_integrals, row_blocks, places, y)
        return (block_two, block_three, hole_term, *sums("plain", 2, [almost], none, [e_near, o_near], ends, []))

    block_two, block_three, hole_term, near_one, near_two = stage(work4)
    ladder_term = assemble(g, near_one, sibling(near_two), block_two, block_three)
    return ladder_term, hole_term


def solution(mesh):
    placed = (P(("gz", "gy"), "gx"), P("gx", ("gy", "gz")), P("gz", None), P(("gz", "gy")), P("gx"))
    sizes = tuple(mesh.shape[name] for name in ("gx", "gy", "gz"))
    return jax.shard_map(
        line_of_four if sizes == (4, 2, 4) else whole_sums,
        mesh=mesh,
        in_specs=placed,
        out_specs=(P(("gz", "gx"), "gy"), P("gz", ("gx", "gy"))),
        check_vma=False,
    )
```

```python
import functools

import jax
import jax.numpy as jnp
from jax import lax
from jax.experimental import pallas as pl
from jax.experimental.pallas import tpu as pltpu
from jax.sharding import PartitionSpec as P

F32 = jnp.float32
CODE = jnp.int16
TAIL = 16
FINE = 64.0
LOG_TOP = 29.9
SMALLEST = 1e-27


def coded(value):
    largest = jnp.maximum(jnp.max(jnp.abs(value)), SMALLEST)
    level = jnp.ceil(jnp.log2(jnp.full((TAIL, value.shape[1]), largest, F32)) * FINE)
    factor = jnp.exp2(LOG_TOP - level[:1] * (1.0 / FINE))
    size = jnp.abs(value) * factor
    size = (size * lax.rsqrt(jnp.maximum(size, 1e-6)) + 0.5).astype(jnp.int32)
    return jnp.where(value < 0.0, -size, size).astype(CODE), level.astype(jnp.int32).astype(CODE)


def decoded(ref, rows):
    code = ref[:rows, :].astype(jnp.int32).astype(F32)
    level = ref[rows:, :].astype(jnp.int32).astype(F32)[:1]
    return code * jnp.abs(code) * jnp.exp2(level * (1.0 / FINE) - LOG_TOP)


def write_coded(ref, value, start, width):
    rows = value.shape[0]
    code, level = coded(value)
    ref[:rows, start:start + width] = code
    ref[rows:, start:start + width] = level


def products_kernel(options, flag_ref, *refs):
    count, inputs = len(options), 2 * sum(options)
    rows_refs, integrals_ref = refs[:inputs], refs[inputs]
    out_refs, code_refs = refs[-2 * count:-count], refs[-count:]
    rows, cols = 2 * rows_refs[0].shape[0], integrals_ref.shape[1]
    width = min(cols, 512)
    step, last = pl.program_id(0), pl.num_programs(0) - 1

    @pl.when(step == 0)
    def _():
        for out_ref in out_refs:
            out_ref[...] = jnp.zeros_like(out_ref)

    blocks, at = [], 0
    for option in options:
        pair = [rows_ref[...] for rows_ref in rows_refs[at:at + 2]]
        if option == 2:
            pair = [jnp.where(flag_ref[0] == 1, one, rows_refs[at + 2 + i][...]) for i, one in enumerate(pair)]
        blocks += pair
        at += 2 * option
    gathered = jnp.concatenate(blocks, axis=0)
    for start in range(0, cols, width):
        value = jnp.dot(gathered, integrals_ref[:, start:start + width], preferred_element_type=F32)
        for index, out_ref in enumerate(out_refs):
            out_ref[:, start:start + width] += value[rows * index:rows * (index + 1)]

    @pl.when(step == last)
    def _():
        for out_ref, code_ref in zip(out_refs, code_refs):
            for start in range(0, cols, width):
                write_coded(code_ref, out_ref[:, start:start + width], start, width)


def products(groups, integrals, flag):
    part, depth = groups[0][0][0].shape
    options, cols = [len(group) for group in groups], integrals.shape[1]
    blocks = [block for group in groups for pair in group for block in pair]
    block, count, rows = min(depth, 1024), len(groups), 2 * part
    results = pl.pallas_call(
        functools.partial(products_kernel, options),
        grid_spec=pltpu.PrefetchScalarGridSpec(
            num_scalar_prefetch=1,
            grid=(depth // block,),
            in_specs=[pl.BlockSpec((part, block), lambda k, _: (0, k))] * len(blocks)
            + [pl.BlockSpec((block, cols), lambda k, _: (k, 0))],
            out_specs=[pl.BlockSpec((rows, cols), lambda k, _: (0, 0))] * count
            + [pl.BlockSpec((rows + TAIL, cols), lambda k, _: (0, 0))] * count,
        ),
        out_shape=[jax.ShapeDtypeStruct((rows, cols), F32)] * count
        + [jax.ShapeDtypeStruct((rows + TAIL, cols), CODE)] * count,
        compiler_params=pltpu.CompilerParams(vmem_limit_bytes=48 << 20),
        cost_estimate=pl.CostEstimate(flops=1_000_000, bytes_accessed=1_000_000, transcendentals=0),
    )(flag.astype(jnp.int32).reshape(1), *blocks, integrals)
    return list(zip(results[:count], results[count:]))


def sums_kernel(kind, outs, bases, choices, arrivals, flags_ref, *refs):
    base_refs, refs = refs[:bases], refs[bases:]
    choice_refs, refs = refs[:choices], refs[choices:]
    arrival_refs, out_refs, total_ref = refs[:arrivals], refs[-1 - outs:-1], refs[-1]
    rows, width = total_ref.shape
    for index, base_ref in enumerate(base_refs):

        @pl.when(flags_ref[0] == index)
        def _():
            total_ref[...] = base_ref[...]

    for index, choice_ref in enumerate(choice_refs):

        @pl.when(flags_ref[1] == index)
        def _():
            total_ref[...] += decoded(choice_ref, rows)

    total = total_ref[...]
    for arrival_ref in arrival_refs:
        total += decoded(arrival_ref, rows)
    each = rows // len(out_refs)
    for index, out_ref in enumerate(out_refs):
        own = total[each * index:each * (index + 1)]
        if kind == "plain":
            out_ref[...] = own
        else:
            write_coded(out_ref, own, 0, width)


def sums(kind, outs, bases, base, choices, choice, arrivals, after=()):
    rows, cols = bases[0].shape
    width = min(cols, 512)
    each = rows // outs + (0 if kind == "plain" else TAIL)
    return pl.pallas_call(
        functools.partial(sums_kernel, kind, outs, len(bases), len(choices), len(arrivals)),
        grid_spec=pltpu.PrefetchScalarGridSpec(
            num_scalar_prefetch=1,
            grid=(cols // width,),
            in_specs=[pl.BlockSpec((rows, width), lambda j, _: (0, j))] * len(bases)
            + [pl.BlockSpec((rows + TAIL, width), lambda j, _: (0, j))] * (len(choices) + len(arrivals))
            + [pl.BlockSpec(memory_space=pl.ANY)] * len(after),
            out_specs=[pl.BlockSpec((each, width), lambda j, _: (0, j))] * outs,
            scratch_shapes=[pltpu.VMEM((rows, width), F32)],
        ),
        out_shape=[jax.ShapeDtypeStruct((each, cols), F32 if kind == "plain" else CODE)] * outs,
        compiler_params=pltpu.CompilerParams(vmem_limit_bytes=24 << 20),
        cost_estimate=pl.CostEstimate(flops=1_000_000, bytes_accessed=1_000_000, transcendentals=0),
    )(jnp.stack([base, choice]).astype(jnp.int32), *bases, *choices, *arrivals, *after)


def assemble_kernel(place_ref, own_ref, sibling_ref, *refs):
    coded_refs, out_ref = refs[:-1], refs[-1]
    flip = pl.program_id(0) ^ place_ref[0]

    @pl.when(flip == 0)
    def _():
        out_ref[...] = own_ref[...]

    @pl.when(flip == 1)
    def _():
        out_ref[...] = sibling_ref[...]

    for index, coded_ref in enumerate(coded_refs):

        @pl.when(flip == 2 + index)
        def _():
            out_ref[...] = decoded(coded_ref, out_ref.shape[0])


def assemble(place, own, sibling, *others):
    rows, cols = own.shape
    return pl.pallas_call(
        assemble_kernel,
        grid_spec=pltpu.PrefetchScalarGridSpec(
            num_scalar_prefetch=1,
            grid=(4,),
            in_specs=[pl.BlockSpec((rows, cols), lambda j, _: (0, 0))] * 2
            + [pl.BlockSpec((rows + TAIL, cols), lambda j, _: (0, 0))] * 2,
            out_specs=pl.BlockSpec((rows, cols), lambda j, _: (0, j)),
        ),
        out_shape=jax.ShapeDtypeStruct((rows, 4 * cols), F32),
        compiler_params=pltpu.CompilerParams(vmem_limit_bytes=24 << 20),
        cost_estimate=pl.CostEstimate(flops=1_000_000, bytes_accessed=1_000_000, transcendentals=0),
    )(place.astype(jnp.int32).reshape(1), own, sibling, *others)


def hole_kernel(count, places_ref, *refs):
    rows_refs, occ_ref = refs[:count], refs[count]
    out_ref, columns_ref = refs[-2:]
    part = rows_refs[0].shape[0]
    for index, rows_ref in enumerate(rows_refs):
        start = pl.multiple_of(places_ref[index] * part, part)
        columns_ref[pl.ds(start, part), :] = rows_ref[...]
    out_ref[...] = jnp.dot(occ_ref[...], columns_ref[...], preferred_element_type=F32)


def hole_product(occ, row_blocks, places, half):
    part, depth = row_blocks[0].shape
    cols = depth // 2
    width = min(cols, 512)
    steps = cols // width
    return pl.pallas_call(
        functools.partial(hole_kernel, len(row_blocks)),
        grid_spec=pltpu.PrefetchScalarGridSpec(
            num_scalar_prefetch=1,
            grid=(steps,),
            in_specs=[pl.BlockSpec((part, width), lambda j, scalars: (0, scalars[len(row_blocks)] * steps + j))] * len(row_blocks)
            + [pl.BlockSpec(occ.shape, lambda j, scalars: (0, 0))],
            out_specs=pl.BlockSpec((occ.shape[0], width), lambda j, scalars: (0, j)),
            scratch_shapes=[pltpu.VMEM((occ.shape[1], width), occ.dtype)],
        ),
        out_shape=jax.ShapeDtypeStruct((occ.shape[0], cols), F32),
        compiler_params=pltpu.CompilerParams(vmem_limit_bytes=24 << 20),
        cost_estimate=pl.CostEstimate(flops=1_000_000, bytes_accessed=1_000_000, transcendentals=0),
    )(jnp.stack([*places, half]).astype(jnp.int32), *row_blocks, occ)


def masked_rows(amplitudes, occ_irrep, virt_irrep):
    keep = occ_irrep[:, None] == virt_irrep[None, :]
    return jnp.where(keep, amplitudes, jnp.zeros_like(amplitudes))


def whole_sums(amplitudes, virt_integrals, occ_integrals, occ_irrep, virt_irrep):
    masked = masked_rows(amplitudes, occ_irrep, virt_irrep)
    rows = lax.all_gather(masked, ("gz", "gy"), axis=0, tiled=True)
    partial = jnp.dot(rows, virt_integrals, preferred_element_type=F32)
    nx, nz = lax.axis_size("gx"), lax.axis_size("gz")
    by_owner = partial.reshape(nz, nx, -1, partial.shape[1]).swapaxes(0, 1)
    mine = lax.psum_scatter(by_owner, "gx", scatter_dimension=0, tiled=True)
    ladder_term = lax.all_to_all(mine[0], "gz", split_axis=0, concat_axis=2, tiled=True)[0]
    width = rows.shape[1] // lax.axis_size("gy")
    columns = lax.dynamic_slice_in_dim(rows, lax.axis_index("gy") * width, width, 1)
    hole_term = jnp.dot(occ_integrals, columns, preferred_element_type=F32)
    return ladder_term, hole_term


def line_of_four(amplitudes, virt_integrals, occ_integrals, occ_irrep, virt_irrep):
    z, y, g = (lax.axis_index(name) for name in ("gx", "gy", "gz"))
    mirrored = z >= 2
    first = (y == 1) != mirrored
    inner = (z == 1) | (z == 2)
    part = amplitudes.shape[0] // 2

    def over_gz(value, flip):
        return lax.ppermute(value, "gz", [(i, i ^ flip) for i in range(4)])

    def sibling(value):
        return over_gz(value, 1)

    def over_gy(value):
        return lax.ppermute(value, "gy", [(0, 1), (1, 0)])

    def inward(code):
        return lax.ppermute(code, "gx", [(0, 1), (3, 2)])

    def across(code):
        return lax.ppermute(code, "gx", [(1, 2), (2, 1)])

    def inward_two(code):
        return lax.ppermute(code, "gx", [(0, 2), (3, 1)])

    def outward_two(code):
        return lax.ppermute(code, "gx", [(1, 3), (2, 0)])

    def outward(code):
        return lax.ppermute(code, "gx", [(2, 3), (1, 0)])

    def own_part(start):
        rows = lax.dynamic_slice_in_dim(amplitudes, start, part, 0)
        labels = lax.dynamic_slice_in_dim(occ_irrep, start, part, 0)
        return masked_rows(rows, labels, virt_irrep)

    def pick(condition, one, other):
        return jnp.where(condition, one, other)

    def stage(work):
        skipped = jax.tree.map(lambda leaf: jnp.zeros(leaf.shape, leaf.dtype), jax.eval_shape(work))
        return lax.cond(z < 4, work, lambda: skipped)

    def times(*groups):
        return products(groups, virt_integrals, first)

    second = ~first
    none = jnp.int32(0)

    def plus(choices, bases, after=()):
        which = second if len(bases) == 2 else none
        return sums("coded", 1, bases, which, choices, which, [], after)[0]

    odd = pick(mirrored, 0, part)
    high = own_part(odd)

    def work0():
        x_high, y_high, s_high = over_gz(high, 2), over_gy(high), sibling(high)
        (near,) = times([(high, s_high)])
        return x_high, y_high, s_high, near, own_part(part - odd)

    x_high, y_high, s_high, (q_near, p0), low = stage(work0)

    def work1():
        a0, yx_high, y_low = inward(p0), over_gz(y_high, 2), over_gy(low)
        sx_high, sy_high = sibling(x_high), sibling(y_high)
        ((q_after, p1),) = times([(x_high, sx_high), (y_high, sy_high)])
        a1, syx_high = inward(p1), sibling(yx_high)
        two, zero = pick(first, low, y_low), pick(first, y_low, low)
        x_two, s_two = over_gz(two, 2), sibling(two)
        third, (_, p5) = times([(y_high, sy_high), (yx_high, syx_high)], [(two, s_two)])
        return a0, a1, yx_high, sx_high, sy_high, syx_high, two, zero, x_two, s_two, q_after, third, p5

    a0, a1, yx_high, sx_high, sy_high, syx_high, two, zero, x_two, s_two, q_after, (q_third, p2), p5 = stage(work1)

    def work2():
        a2, m_near, x_zero, sx_two, s_zero = inward(p2), across(p5), over_gz(zero, 2), sibling(x_two), sibling(zero)
        ((q_two_far, p3),) = times([(x_two, sx_two)])
        a3, b0 = inward(p3), outward_two(plus([a0, a1], [q_near, q_after], [p3]))
        (rest,) = times([(yx_high, syx_high), (x_high, sx_high)])
        b1 = plus([a1, a2], [q_after, q_third])
        return a2, m_near, x_zero, sx_two, s_zero, a3, b0, rest, b1, q_two_far

    a2, m_near, x_zero, sx_two, s_zero, a3, b0, (q_rest, p4), p_b1, q_two_far = stage(work2)
    def work3():
        a4, b1, sx_zero = inward(p4), outward_two(p_b1), sibling(x_zero)
        b2 = plus([a3], [q_two_far])
        (zero_far,) = times([(x_zero, sx_zero)])
        return a4, b1, sx_zero, b2, zero_far

    a4, b1, sx_zero, p_b2, (q_zero_far, p6) = stage(work3)
    ends = pick(inner, 0, 1)

    def work4():
        b2, o_far = across(p_b2), outward(p6)
        (zero_near,) = times([(zero, s_zero)])
        (far,) = sums("plain", 1, [q_rest, q_zero_far], ends, [a4, b1], ends, [])
        return zero_near, sums("coded", 2, [far], none, [b2, o_far], ends, [])

    (q_zero_near, p7), (far_one, far_two) = stage(work4)

    def owner(index):
        return pick(mirrored, 3 - index, index)

    held = (
        (owner(pick(first, 3, 1)), (high, s_high, x_high, sx_high)),
        (owner(pick(first, 1, 3)), (y_high, sy_high, yx_high, syx_high)),
        (owner(2), (two, s_two, x_two, sx_two)),
        (owner(0), (zero, s_zero, x_zero, sx_zero)),
    )
    row_blocks = [block for _, group in held for block in group]
    places = [(g ^ flip) * 4 + place for place, _ in held for flip in range(4)]

    def work5():
        e_near, o_near, block_two, block_three = inward_two(p5), outward(p7), over_gz(far_one, 2), over_gz(far_two, 3)
        base = pick(inner, pick(first, 0, 1), 2)
        (almost,) = sums("plain", 1, [q_third, q_near, q_zero_near], base, [a2, a0, b0], base, [m_near])
        hole_term = hole_product(occ_integrals, row_blocks, places, y)
        return (block_two, block_three, hole_term, *sums("plain", 2, [almost], none, [e_near, o_near], ends, []))

    block_two, block_three, hole_term, near_one, near_two = stage(work5)
    ladder_term = assemble(g, near_one, sibling(near_two), block_two, block_three)
    return ladder_term, hole_term


def solution(mesh):
    placed = (P(("gz", "gy"), "gx"), P("gx", ("gy", "gz")), P("gz", None), P(("gz", "gy")), P("gx"))
    sizes = tuple(mesh.shape[name] for name in ("gx", "gy", "gz"))
    return jax.shard_map(
        line_of_four if sizes == (4, 2, 4) else whole_sums,
        mesh=mesh,
        in_specs=placed,
        out_specs=(P(("gz", "gx"), "gy"), P("gz", ("gx", "gy"))),
        check_vma=False,
    )
```

```python
import functools

import jax
import jax.numpy as jnp
from jax import lax
from jax.experimental import pallas as pl
from jax.experimental.pallas import tpu as pltpu
from jax.sharding import PartitionSpec as P

F32 = jnp.float32
CODE = jnp.int16
TAIL = 16
FINE = 64.0
LOG_TOP = 29.9
SMALLEST = 1e-27


def coded(value):
    largest = jnp.maximum(jnp.max(jnp.abs(value)), SMALLEST)
    level = jnp.ceil(jnp.log2(jnp.full((TAIL, value.shape[1]), largest, F32)) * FINE)
    factor = jnp.exp2(LOG_TOP - level[:1] * (1.0 / FINE))
    size = jnp.abs(value) * factor
    size = (size * lax.rsqrt(jnp.maximum(size, 1e-6)) + 0.5).astype(jnp.int32)
    return jnp.where(value < 0.0, -size, size).astype(CODE), level.astype(jnp.int32).astype(CODE)


def decoded(ref, rows):
    code = ref[:rows, :].astype(jnp.int32).astype(F32)
    level = ref[rows:, :].astype(jnp.int32).astype(F32)[:1]
    return code * jnp.abs(code) * jnp.exp2(level * (1.0 / FINE) - LOG_TOP)


def write_coded(ref, value, start, width):
    rows = value.shape[0]
    code, level = coded(value)
    ref[:rows, start:start + width] = code
    ref[rows:, start:start + width] = level


def products_kernel(options, flag_ref, *refs):
    count, inputs = len(options), 2 * sum(options)
    rows_refs, integrals_ref = refs[:inputs], refs[inputs]
    out_refs, code_refs = refs[-2 * count:-count], refs[-count:]
    rows, cols = 2 * rows_refs[0].shape[0], integrals_ref.shape[1]
    width = min(cols, 512)
    step, last = pl.program_id(0), pl.num_programs(0) - 1

    @pl.when(step == 0)
    def _():
        for out_ref in out_refs:
            out_ref[...] = jnp.zeros_like(out_ref)

    blocks, at = [], 0
    for option in options:
        pair = [rows_ref[...] for rows_ref in rows_refs[at:at + 2]]
        if option == 2:
            pair = [jnp.where(flag_ref[0] == 1, one, rows_refs[at + 2 + i][...]) for i, one in enumerate(pair)]
        blocks += pair
        at += 2 * option
    gathered = jnp.concatenate(blocks, axis=0)
    for start in range(0, cols, width):
        value = jnp.dot(gathered, integrals_ref[:, start:start + width], preferred_element_type=F32)
        for index, out_ref in enumerate(out_refs):
            out_ref[:, start:start + width] += value[rows * index:rows * (index + 1)]

    @pl.when(step == last)
    def _():
        for out_ref, code_ref in zip(out_refs, code_refs):
            for start in range(0, cols, width):
                write_coded(code_ref, out_ref[:, start:start + width], start, width)


def products(groups, integrals, flag):
    part, depth = groups[0][0][0].shape
    options, cols = [len(group) for group in groups], integrals.shape[1]
    blocks = [block for group in groups for pair in group for block in pair]
    block, count, rows = min(depth, 1024), len(groups), 2 * part
    results = pl.pallas_call(
        functools.partial(products_kernel, options),
        grid_spec=pltpu.PrefetchScalarGridSpec(
            num_scalar_prefetch=1,
            grid=(depth // block,),
            in_specs=[pl.BlockSpec((part, block), lambda k, _: (0, k))] * len(blocks)
            + [pl.BlockSpec((block, cols), lambda k, _: (k, 0))],
            out_specs=[pl.BlockSpec((rows, cols), lambda k, _: (0, 0))] * count
            + [pl.BlockSpec((rows + TAIL, cols), lambda k, _: (0, 0))] * count,
        ),
        out_shape=[jax.ShapeDtypeStruct((rows, cols), F32)] * count
        + [jax.ShapeDtypeStruct((rows + TAIL, cols), CODE)] * count,
        compiler_params=pltpu.CompilerParams(vmem_limit_bytes=48 << 20),
        cost_estimate=pl.CostEstimate(flops=1_000_000, bytes_accessed=1_000_000, transcendentals=0),
    )(flag.astype(jnp.int32).reshape(1), *blocks, integrals)
    return list(zip(results[:count], results[count:]))


def sums_kernel(kind, outs, bases, choices, arrivals, flags_ref, *refs):
    base_refs, refs = refs[:bases], refs[bases:]
    choice_refs, refs = refs[:choices], refs[choices:]
    arrival_refs, out_refs, total_ref = refs[:arrivals], refs[-1 - outs:-1], refs[-1]
    rows, width = total_ref.shape
    for index, base_ref in enumerate(base_refs):

        @pl.when(flags_ref[0] == index)
        def _():
            total_ref[...] = base_ref[...]

    for index, choice_ref in enumerate(choice_refs):

        @pl.when(flags_ref[1] == index)
        def _():
            total_ref[...] += decoded(choice_ref, rows)

    total = total_ref[...]
    for arrival_ref in arrival_refs:
        total += decoded(arrival_ref, rows)
    each = rows // len(out_refs)
    for index, out_ref in enumerate(out_refs):
        own = total[each * index:each * (index + 1)]
        if kind == "plain":
            out_ref[...] = own
        else:
            write_coded(out_ref, own, 0, width)


def sums(kind, outs, bases, base, choices, choice, arrivals):
    rows, cols = bases[0].shape
    width = min(cols, 512)
    each = rows // outs + (0 if kind == "plain" else TAIL)
    return pl.pallas_call(
        functools.partial(sums_kernel, kind, outs, len(bases), len(choices), len(arrivals)),
        grid_spec=pltpu.PrefetchScalarGridSpec(
            num_scalar_prefetch=1,
            grid=(cols // width,),
            in_specs=[pl.BlockSpec((rows, width), lambda j, _: (0, j))] * len(bases)
            + [pl.BlockSpec((rows + TAIL, width), lambda j, _: (0, j))] * (len(choices) + len(arrivals)),
            out_specs=[pl.BlockSpec((each, width), lambda j, _: (0, j))] * outs,
            scratch_shapes=[pltpu.VMEM((rows, width), F32)],
        ),
        out_shape=[jax.ShapeDtypeStruct((each, cols), F32 if kind == "plain" else CODE)] * outs,
        compiler_params=pltpu.CompilerParams(vmem_limit_bytes=24 << 20),
        cost_estimate=pl.CostEstimate(flops=1_000_000, bytes_accessed=1_000_000, transcendentals=0),
    )(jnp.stack([base, choice]).astype(jnp.int32), *bases, *choices, *arrivals)


def assemble_kernel(place_ref, own_ref, sibling_ref, *refs):
    coded_refs, out_ref = refs[:-1], refs[-1]
    flip = pl.program_id(0) ^ place_ref[0]

    @pl.when(flip == 0)
    def _():
        out_ref[...] = own_ref[...]

    @pl.when(flip == 1)
    def _():
        out_ref[...] = sibling_ref[...]

    for index, coded_ref in enumerate(coded_refs):

        @pl.when(flip == 2 + index)
        def _():
            out_ref[...] = decoded(coded_ref, out_ref.shape[0])


def assemble(place, own, sibling, *others):
    rows, cols = own.shape
    return pl.pallas_call(
        assemble_kernel,
        grid_spec=pltpu.PrefetchScalarGridSpec(
            num_scalar_prefetch=1,
            grid=(4,),
            in_specs=[pl.BlockSpec((rows, cols), lambda j, _: (0, 0))] * 2
            + [pl.BlockSpec((rows + TAIL, cols), lambda j, _: (0, 0))] * 2,
            out_specs=pl.BlockSpec((rows, cols), lambda j, _: (0, j)),
        ),
        out_shape=jax.ShapeDtypeStruct((rows, 4 * cols), F32),
        compiler_params=pltpu.CompilerParams(vmem_limit_bytes=24 << 20),
        cost_estimate=pl.CostEstimate(flops=1_000_000, bytes_accessed=1_000_000, transcendentals=0),
    )(place.astype(jnp.int32).reshape(1), own, sibling, *others)


def hole_kernel(count, places_ref, *refs):
    rows_refs, occ_ref = refs[:count], refs[count]
    out_ref, columns_ref = refs[-2:]
    part = rows_refs[0].shape[0]
    for index, rows_ref in enumerate(rows_refs):
        start = pl.multiple_of(places_ref[index] * part, part)
        columns_ref[pl.ds(start, part), :] = rows_ref[...]
    out_ref[...] = jnp.dot(occ_ref[...], columns_ref[...], preferred_element_type=F32)


def hole_product(occ, row_blocks, places, half):
    part, depth = row_blocks[0].shape
    cols = depth // 2
    width = min(cols, 512)
    steps = cols // width
    return pl.pallas_call(
        functools.partial(hole_kernel, len(row_blocks)),
        grid_spec=pltpu.PrefetchScalarGridSpec(
            num_scalar_prefetch=1,
            grid=(steps,),
            in_specs=[pl.BlockSpec((part, width), lambda j, scalars: (0, scalars[len(row_blocks)] * steps + j))] * len(row_blocks)
            + [pl.BlockSpec(occ.shape, lambda j, scalars: (0, 0))],
            out_specs=pl.BlockSpec((occ.shape[0], width), lambda j, scalars: (0, j)),
            scratch_shapes=[pltpu.VMEM((occ.shape[1], width), occ.dtype)],
        ),
        out_shape=jax.ShapeDtypeStruct((occ.shape[0], cols), F32),
        compiler_params=pltpu.CompilerParams(vmem_limit_bytes=24 << 20),
        cost_estimate=pl.CostEstimate(flops=1_000_000, bytes_accessed=1_000_000, transcendentals=0),
    )(jnp.stack([*places, half]).astype(jnp.int32), *row_blocks, occ)


def masked_rows(amplitudes, occ_irrep, virt_irrep):
    keep = occ_irrep[:, None] == virt_irrep[None, :]
    return jnp.where(keep, amplitudes, jnp.zeros_like(amplitudes))


def whole_sums(amplitudes, virt_integrals, occ_integrals, occ_irrep, virt_irrep):
    masked = masked_rows(amplitudes, occ_irrep, virt_irrep)
    rows = lax.all_gather(masked, ("gz", "gy"), axis=0, tiled=True)
    partial = jnp.dot(rows, virt_integrals, preferred_element_type=F32)
    nx, nz = lax.axis_size("gx"), lax.axis_size("gz")
    by_owner = partial.reshape(nz, nx, -1, partial.shape[1]).swapaxes(0, 1)
    mine = lax.psum_scatter(by_owner, "gx", scatter_dimension=0, tiled=True)
    ladder_term = lax.all_to_all(mine[0], "gz", split_axis=0, concat_axis=2, tiled=True)[0]
    width = rows.shape[1] // lax.axis_size("gy")
    columns = lax.dynamic_slice_in_dim(rows, lax.axis_index("gy") * width, width, 1)
    hole_term = jnp.dot(occ_integrals, columns, preferred_element_type=F32)
    return ladder_term, hole_term


def line_of_four(amplitudes, virt_integrals, occ_integrals, occ_irrep, virt_irrep):
    z, y, g = (lax.axis_index(name) for name in ("gx", "gy", "gz"))
    mirrored = z >= 2
    first = (y == 1) != mirrored
    inner = (z == 1) | (z == 2)
    part = amplitudes.shape[0] // 2

    def over_gz(value, flip):
        return lax.ppermute(value, "gz", [(i, i ^ flip) for i in range(4)])

    def sibling(value):
        return over_gz(value, 1)

    def over_gy(value):
        return lax.ppermute(value, "gy", [(0, 1), (1, 0)])

    def inward(code):
        return lax.ppermute(code, "gx", [(0, 1), (3, 2)])

    def across(code):
        return lax.ppermute(code, "gx", [(1, 2), (2, 1)])

    def inward_and_out(code):
        return lax.ppermute(code, "gx", [(0, 1), (3, 2), (1, 3), (2, 0)])

    def outward_and_in(code):
        return lax.ppermute(code, "gx", [(1, 0), (2, 3), (0, 2), (3, 1)])

    def outward(code):
        return lax.ppermute(code, "gx", [(2, 3), (1, 0)])

    def own_part(start):
        rows = lax.dynamic_slice_in_dim(amplitudes, start, part, 0)
        labels = lax.dynamic_slice_in_dim(occ_irrep, start, part, 0)
        return masked_rows(rows, labels, virt_irrep)

    def pick(condition, one, other):
        return jnp.where(condition, one, other)

    def stage(work):
        skipped = jax.tree.map(lambda leaf: jnp.zeros(leaf.shape, leaf.dtype), jax.eval_shape(work))
        return lax.cond(z < 4, work, lambda: skipped)

    def times(*groups):
        return products(groups, virt_integrals, first)

    second = ~first
    none = jnp.int32(0)

    def plus(choices, bases):
        which = second if len(bases) == 2 else none
        return sums("coded", 1, bases, which, choices, which, [])[0]

    odd = pick(mirrored, 0, part)
    high = own_part(odd)

    def work0():
        x_high, y_high, s_high = over_gz(high, 2), over_gy(high), sibling(high)
        (near,) = times([(high, s_high)])
        return x_high, y_high, s_high, near, own_part(part - odd)

    x_high, y_high, s_high, (q_near, p0), low = stage(work0)

    def work1():
        a0, yx_high, y_low = inward(p0), over_gz(y_high, 2), over_gy(low)
        sx_high, sy_high = sibling(x_high), sibling(y_high)
        ((q_after, p1),) = times([(x_high, sx_high), (y_high, sy_high)])
        a1, syx_high = inward(p1), sibling(yx_high)
        two, zero = pick(first, low, y_low), pick(first, y_low, low)
        x_two, s_two = over_gz(two, 2), sibling(two)
        third, (_, p5) = times([(y_high, sy_high), (yx_high, syx_high)], [(two, s_two)])
        return a0, a1, yx_high, sx_high, sy_high, syx_high, two, zero, x_two, s_two, q_after, third, p5

    a0, a1, yx_high, sx_high, sy_high, syx_high, two, zero, x_two, s_two, q_after, (q_third, p2), p5 = stage(work1)

    def work2():
        a2, m_near, x_zero, sx_two, s_zero = inward(p2), across(p5), over_gz(zero, 2), sibling(x_two), sibling(zero)
        ((q_two_far, p3),) = times([(x_two, sx_two)])
        b0 = plus([a0, a1], [q_near, q_after])
        a3_b0 = inward_and_out(pick(inner, b0, p3))
        ((q_rest, p4),) = times([(yx_high, syx_high), (x_high, sx_high)])
        b1 = plus([a1, a2], [q_after, q_third])
        return a2, m_near, x_zero, sx_two, s_zero, a3_b0, q_rest, pick(inner, b1, p4), q_two_far

    a2, m_near, x_zero, sx_two, s_zero, a3_b0, q_rest, p_a4_b1, q_two_far = stage(work2)
    def work3():
        a4_b1, sx_zero = inward_and_out(p_a4_b1), sibling(x_zero)
        b2 = plus([a3_b0], [q_two_far])
        (zero_far,) = times([(x_zero, sx_zero)])
        return a4_b1, sx_zero, b2, zero_far

    a4_b1, sx_zero, p_b2, (q_zero_far, p6) = stage(work3)
    ends = pick(inner, 0, 1)

    def work4():
        b2, o_far = across(p_b2), outward(p6)
        ((zero_near, p7),) = times([(zero, s_zero)])
        (far,) = sums("plain", 1, [q_rest, q_zero_far], ends, [], none, [a4_b1])
        return zero_near, pick(inner, p7, p5), sums("coded", 2, [far], none, [b2, o_far], ends, [])

    q_zero_near, p_last, (far_one, far_two) = stage(work4)

    def owner(index):
        return pick(mirrored, 3 - index, index)

    held = (
        (owner(pick(first, 3, 1)), (high, s_high, x_high, sx_high)),
        (owner(pick(first, 1, 3)), (y_high, sy_high, yx_high, syx_high)),
        (owner(2), (two, s_two, x_two, sx_two)),
        (owner(0), (zero, s_zero, x_zero, sx_zero)),
    )
    row_blocks = [block for _, group in held for block in group]
    places = [(g ^ flip) * 4 + place for place, _ in held for flip in range(4)]

    def work5():
        last, block_two, block_three = outward_and_in(p_last), over_gz(far_one, 2), over_gz(far_two, 3)
        base = pick(inner, pick(first, 0, 1), 2)
        (almost,) = sums("plain", 1, [q_third, q_near, q_zero_near], base, [a2, a0, a3_b0], base, [m_near])
        hole_term = hole_product(occ_integrals, row_blocks, places, y)
        return (block_two, block_three, hole_term, *sums("plain", 2, [almost], none, [], none, [last]))

    block_two, block_three, hole_term, near_one, near_two = stage(work5)
    ladder_term = assemble(g, near_one, sibling(near_two), block_two, block_three)
    return ladder_term, hole_term


def solution(mesh):
    placed = (P(("gz", "gy"), "gx"), P("gx", ("gy", "gz")), P("gz", None), P(("gz", "gy")), P("gx"))
    sizes = tuple(mesh.shape[name] for name in ("gx", "gy", "gz"))
    return jax.shard_map(
        line_of_four if sizes == (4, 2, 4) else whole_sums,
        mesh=mesh,
        in_specs=placed,
        out_specs=(P(("gz", "gx"), "gy"), P("gz", ("gx", "gy"))),
        check_vma=False,
    )
```
